32 devices in a mesh: layer: 4 (over x, core), doc: 8 (over z, y).
Axes of the slice: x: 2, y: 2, z: 4, core: 2. Of those that a mesh axis runs over, the one named last changes fastest.
Arguments:
- query_grads: bfloat16 [4, 256, 4096], P('layer', 'doc'), may hold values from -6 to 6
- stored_grads: bfloat16 [4, 8192, 4096], P('layer', 'doc'), may hold values from -0.0234375 to 0.0234375
- basis_in: float32 [4, 64, 64], P('layer'), may hold values from -0.75 to 0.75
- basis_out: float32 [4, 64, 64], P('layer'), may hold values from -0.75 to 0.75
- eigen_values: float32 [4, 64, 64], P('layer'), may hold values from 0.02 to 4
- layer_mask: int32 [256, 4], P(None, 'layer'), may hold values 0 or 1
- doc_counts: int32 [8], P('doc'), may hold values from 1 to 1024, 4096 in all
Outputs:
- scores: float32 [256, 8192], P('layer', 'doc')
The draws below stay inside these ranges and needn't reach their ends.
Inputs may be any that keep to these rules, and one draw needn't show every extreme that they name: `doc_counts`: the counts sum to 4096 and the largest equals 1024.
All inputs are finite; a program needn't handle non-finite values. No bound on the sum of `layer_mask` or of `doc_counts` on one device may be relied on, other than what follows from the above.
Results may differ from the reference program's by a relative error of at most 0.0029.
Values may be sent and summed in bfloat16 or wider, within the bound.
A program may use at most 64 MiB of HBM per device.

```python
import math
import jax
import jax.numpy as jnp
import numpy as np
from jax import lax

A = 64
B = 64
Q = 256
DOC_DEV = 1024
LAYERS = 4
DOC_SHARDS = 8
DOCS = 8192
N_DOC = 8


def touch_ends(array, stream_key, low, largest):
    shape = array.shape
    spot = [jax.random.randint(jax.random.fold_in(stream_key, axis), (), 0, shape[axis]) for axis in range(len(shape))]
    array = array.at[tuple(spot)].set(low)
    longest = shape.index(max(shape))
    spot[longest] = (spot[longest] + 1) % shape[longest]
    return array.at[tuple(spot)].set(largest)


def steps_of(rng, dims, shards, smallest, high):
    def one(dim, parts):
        draws = jax.random.uniform(jax.random.fold_in(jax.random.fold_in(rng, 6), dim), (parts,), jnp.float32, smallest / len(shards), high / len(shards))
        return jnp.repeat(jnp.exp(draws), dims[dim] // parts).reshape((-1,) + (1,) * (len(dims) - dim - 1))

    factor_of = one(*shards[0])
    for cut in shards[1:]:
        factor_of = factor_of * one(*cut)
    return factor_of


def length_profile(amount, total, most, skew):
    portions = [(1 << 20) // math.isqrt(standing ** skew) + 1 for standing in range(2, amount + 1)]
    rest, given = total - most - (amount - 1), [1] * (amount - 1)
    while rest > 0:
        candidates = [i for i in range(amount - 1) if given[i] < most]
        mass, remaining = sum([portions[i] for i in candidates]), rest
        for i in candidates:
            addition = min(most - given[i], max(1, remaining * portions[i] // mass), rest)
            given[i] = given[i] + addition
            rest = rest - addition
    return np.array([most] + given)


def ragged_sizes(key, amount, total, reach, skew):
    if amount == 2:
        one = jax.random.randint(key, (), max(1, total - reach), min(reach, total - 1) + 1)
        return jnp.stack([one, total - one])
    tallies = jnp.asarray(length_profile(amount, total, reach, skew), jnp.int32)
    twos = (amount - 1) // 2
    giver, receiver = tallies[1:1 + 2 * twos:2], tallies[2:2 + 2 * twos:2]
    slack = jnp.minimum(giver - 1, reach - receiver)
    shifted = jax.random.randint(jax.random.fold_in(key, 1), (twos,), 0, 1 << 20) % (slack + 1)
    tallies = tallies.at[1:1 + 2 * twos:2].set(giver - shifted).at[2:2 + 2 * twos:2].set(receiver + shifted)
    return tallies[jax.random.permutation(jax.random.fold_in(key, 2), amount)]


def bell_draw(own_key, shape, spread, reach, pieces=(), kind=jnp.bfloat16):
    values = spread * jax.random.normal(own_key, shape, jnp.float32)
    if pieces:
        values = values * steps_of(own_key, shape, pieces, -0.22, 0.18)
    return jnp.clip(values, -reach, reach).astype(kind)


def setup_inputs(seed: int = 0) -> dict:
    keys = jax.random.split(jax.random.key(seed), 8)
    query_grads = bell_draw(keys[0], (LAYERS, Q, B * A), 1.0, 6.0, ((0, 4), (1, 8)))
    stored_grads = bell_draw(keys[1], (LAYERS, DOCS, B * A), (16 * B * A) ** -0.5, 0.0234375, ((0, 4), (1, 8)))
    basis_in = bell_draw(keys[2], (LAYERS, A, A), A ** -0.5, 0.75, ((0, 4),), jnp.float32)
    basis_out = bell_draw(keys[3], (LAYERS, B, B), B ** -0.5, 0.75, ((0, 4),), jnp.float32)
    eigen_values = jnp.clip(jnp.exp(math.log(4.0) - 5.2983174 * jax.random.uniform(keys[4], (LAYERS, B, A), jnp.float32) ** steps_of(keys[4], (LAYERS, B, A), ((0, 4),), -0.2, 0.2)), 0.02, 4.0)
    layer_mask = touch_ends((jax.random.randint(keys[5], (Q, LAYERS), 0, 4) < 3).astype(jnp.int32), jax.random.fold_in(keys[5], 1), 0, 1)
    doc_counts = ragged_sizes(keys[6], DOC_SHARDS, DOC_DEV * N_DOC // 2, DOC_DEV, 2).astype(jnp.int32)
    return {"query_grads": query_grads, "stored_grads": stored_grads, "basis_in": basis_in, "basis_out": basis_out, "eigen_values": eigen_values, "layer_mask": layer_mask, "doc_counts": doc_counts}


damping = 0.1


def precondition(gradients, basis_in, basis_out, eigen_values):
    row_count = gradients.shape[0]
    grid_blocks = gradients.astype(jnp.float32).reshape(row_count, basis_out.shape[0], basis_in.shape[0])
    rotated = jnp.einsum("xi,qxy,yj->qij", basis_out, grid_blocks, basis_in, precision=lax.Precision.HIGHEST)
    scaled = rotated / (eigen_values + damping)
    restored = jnp.einsum("bi,qij,aj->qba", basis_out, scaled, basis_in, precision=lax.Precision.HIGHEST)
    return restored.reshape(row_count, -1).astype(jnp.bfloat16)


def reference(query_grads, stored_grads, basis_in, basis_out, eigen_values, layer_mask, doc_counts):
    live_slots = (jnp.arange(DOC_DEV, dtype=jnp.int32)[None, :] < doc_counts[:, None]).reshape(-1)

    def one_layer(carry, inputs):
        queries, stored, base_in, base_out, eigens, weights = inputs
        prepared = precondition(queries, base_in, base_out, eigens)
        prepared = prepared * weights.astype(prepared.dtype)[:, None]
        tile = lax.dot_general(prepared, stored, (((1,), (1,)), ((), ())), preferred_element_type=jnp.float32)
        return carry + tile, None

    start_value = jnp.zeros((Q, DOCS), jnp.float32)
    summed, _ = lax.scan(one_layer, start_value, (query_grads, stored_grads, basis_in, basis_out, eigen_values, layer_mask.T))
    return jnp.where(live_slots[None, :], summed, jnp.zeros_like(summed))
```

```python
import functools
import jax
import jax.numpy as jnp
from jax import lax
from jax.experimental import pallas as pl
from jax.experimental.pallas import tpu as pltpu
from jax.sharding import PartitionSpec as P

damping = 0.1
N_CHUNK = 4
MESH = pl.DeviceIdType.MESH
f32 = jnp.float32
bf16 = jnp.bfloat16


def precondition(gradients, basis_in, basis_out, eigen_values):
    row_count = gradients.shape[0]
    grid_blocks = gradients.astype(jnp.float32).reshape(
        row_count, basis_out.shape[0], basis_in.shape[0]
    )
    rotated = jnp.einsum(
        "xi,qxy,yj->qij", basis_out, grid_blocks, basis_in, precision=lax.Precision.HIGHEST
    )
    scaled = rotated / (eigen_values + damping)
    restored = jnp.einsum(
        "bi,qij,aj->qba", basis_out, scaled, basis_in, precision=lax.Precision.HIGHEST
    )
    return restored.reshape(row_count, -1).astype(jnp.bfloat16)


def by_collectives(query_grads, stored_grads, basis_in, basis_out, eigen_values, layer_mask, doc_counts):
    stored = stored_grads[0]
    row_weights = layer_mask[:, 0].astype(jnp.bfloat16)
    own_rows = precondition(query_grads[0], basis_in[0], basis_out[0], eigen_values[0])
    masked = lax.all_gather(own_rows, "doc", axis=0, tiled=True) * row_weights[:, None]
    score_tiles = lax.dot_general(
        masked, stored, (((1,), (1,)), ((), ())), preferred_element_type=jnp.float32
    )
    live_slots = jnp.arange(stored.shape[0], dtype=jnp.int32) < doc_counts[0]
    score_tiles = jnp.where(live_slots[None, :], score_tiles, jnp.zeros_like(score_tiles))
    return lax.psum_scatter(score_tiles, "layer", scatter_dimension=0, tiled=True)


def halves(x):
    hi = x.astype(bf16)
    return hi, (x - hi.astype(f32)).astype(bf16)


def nn(a, b):
    return lax.dot_general(a, b, (((1,), (0,)), ((), ())), preferred_element_type=f32)


def nt(a, b):
    return lax.dot_general(a, b, (((1,), (1,)), ((), ())), preferred_element_type=f32)


def one_hot(hits):
    return jnp.where(hits, 1.0, 0.0).astype(bf16)


def iota(shape, dim):
    return lax.broadcasted_iota(jnp.int32, shape, dim)


def write_own_rows(q_ref, bi_ref, bo_ref, ev_ref, mask_ref, gath, me):
    x = q_ref[0].astype(f32)
    r, c = iota((256, 256), 0), iota((256, 256), 1)
    same = (r // 128 == (c // 64) % 2) & ((r // 64) % 2 == c // 128)
    put_a = one_hot(iota((256, 64), 0) % 64 == iota((256, 64), 1))
    wa = [
        jnp.where(same, nt(nn(put_a, part).astype(bf16), put_a), 0.0).astype(bf16)
        for part in halves(bi_ref[0])
    ]
    row = iota((512, 64), 0)
    put_b = one_hot(2 * ((row // 8) % 32) + row // 256 == iota((512, 64), 1))
    eye = iota((512, 512), 0) % 8 == iota((512, 512), 1) % 8
    wc, wb = [], []
    for part in halves(bo_ref[0]):
        wc.append(jnp.where(eye, nt(nn(put_b, part).astype(bf16), put_b), 0.0).astype(bf16))
        wb.append(jnp.where(eye, nt(nt(put_b, part).astype(bf16), put_b), 0.0).astype(bf16))
    inverse = 1.0 / (ev_ref[0] + damping)
    top, low = halves(inverse)
    low = inverse - top.astype(f32)
    mid, low = halves(low)
    scale = 0.0
    for part in (top, mid, low):
        scale = scale + nt(nn(put_b, part).astype(bf16), put_a)

    turned = []
    for gp in range(2):
        pieces = [
            jnp.concatenate(
                [
                    x[8 * (2 * gp + g) : 8 * (2 * gp + g) + 8, 128 * j : 128 * j + 128]
                    for j in range(32)
                ],
                axis=0,
            )
            for g in range(2)
        ]
        block = jnp.concatenate(pieces, axis=1).astype(bf16)
        turned.append(nn(block, wa[0]) + nn(block, wa[1]))
    s = jnp.concatenate(
        [
            jnp.concatenate([turned[gp][:, 128 * p : 128 * p + 128] for gp in range(2)], axis=1)
            for p in range(2)
        ],
        axis=0,
    )
    s_hi, s_lo = halves(s)
    rotated = nn(wb[0], s_hi) + (nn(wb[0], s_lo) + nn(wb[1], s_hi))
    v_hi, v_lo = halves(rotated * scale)
    v = nn(wc[0], v_hi) + (nn(wc[0], v_lo) + nn(wc[1], v_hi))
    weights = mask_ref[pl.ds(pl.multiple_of(me * 32, 32), 32), :].astype(f32)
    for gp in range(2):
        y = jnp.concatenate(
            [v[256 * p : 256 * p + 256, 128 * gp : 128 * gp + 128] for p in range(2)], axis=1
        )
        y_hi, y_lo = halves(y)
        done = nt(y_hi, wa[0]) + (nt(y_lo, wa[0]) + nt(y_hi, wa[1]))
        w16 = weights[16 * gp : 16 * gp + 16, :]
        rows = pl.ds(pl.multiple_of(me * 32 + 16 * gp, 16), 16)
        for j in range(32):
            tile = jnp.concatenate(
                [done[8 * j : 8 * j + 8, :128], done[8 * j : 8 * j + 8, 128:]], axis=0
            )
            gath[j // 8, rows, 128 * (j % 8) : 128 * (j % 8) + 128] = (tile * w16).astype(bf16)


def kernel(
    nz, q_ref, stored_ref, bi_ref, bo_ref, ev_ref, mask_ref, cnt_ref, out_ref,
    st, gath, acc, sbuf, rbuf,
    st_sem, recv_sem, up_sem, down_sem, y_sem, rs_send, rs_recv,
):
    layers = sbuf.shape[0]
    width = st.shape[2]
    me = lax.axis_index("doc")
    mine = lax.axis_index("layer")
    z, y = me // 2, me % 2
    partner = me + 1 - 2 * y

    def load(k):
        return pltpu.make_async_copy(
            stored_ref.at[0, :, pl.ds(k * width, width)], st.at[k], st_sem.at[k]
        )

    for k in range(N_CHUNK):
        load(k).start()

    barrier = pltpu.get_barrier_semaphore()
    pl.semaphore_signal(barrier, inc=1, device_id={"doc": partner}, device_id_type=MESH)
    for step in range(1, layers):
        pl.semaphore_signal(
            barrier, inc=1, device_id={"layer": lax.rem(mine + step, layers)}, device_id_type=MESH
        )

    @pl.when(z < nz - 1)
    def _():
        pl.semaphore_signal(barrier, inc=1, device_id={"doc": me + 2}, device_id_type=MESH)

    @pl.when(z > 0)
    def _():
        pl.semaphore_signal(barrier, inc=1, device_id={"doc": me - 2}, device_id_type=MESH)

    write_own_rows(q_ref, bi_ref, bo_ref, ev_ref, mask_ref, gath, me)

    ends = jnp.where(z == 0, 1, 0) + jnp.where(z == nz - 1, 1, 0)
    pl.semaphore_wait(barrier, layers + 2 - ends)

    def plane_at(s):
        far = (z >= 2).astype(jnp.int32)
        near = z + far * (3 - 2 * z)
        inner = (near == 1).astype(jnp.int32)
        swap = inner * jnp.where(s < 2, 1, 0)
        p = s + swap * (1 - 2 * s)
        return p + far * (3 - 2 * p)

    def send(p, side, k, sems, target):
        blk = 2 * p + side
        part = gath.at[k, pl.ds(pl.multiple_of(blk * 32, 32), 32)]
        return pltpu.make_async_remote_copy(
            src_ref=part, dst_ref=part, send_sem=sems.at[p, k], recv_sem=recv_sem.at[blk, k],
            device_id={"doc": target}, device_id_type=MESH,
        )

    def forward(t):
        p, k = plane_at(t // N_CHUNK), t % N_CHUNK

        @pl.when(p != z)
        def _():
            send(p, y, k, y_sem, partner).wait_recv()

        @pl.when((p <= z) & (z < nz - 1))
        def _():
            send(p, y, k, up_sem, me + 2).start()

        @pl.when((p >= z) & (z > 0))
        def _():
            send(p, y, k, down_sem, me - 2).start()

        send(p, y, k, y_sem, partner).start()

    def hand_over(p, s):
        return pltpu.make_async_remote_copy(
            src_ref=sbuf.at[s], dst_ref=rbuf.at[mine], send_sem=rs_send.at[s],
            recv_sem=rs_recv.at[mine], device_id={"layer": p}, device_id_type=MESH,
        )

    def compute(t):
        s, k = t // N_CHUNK, t % N_CHUNK
        p = plane_at(s)
        send(p, 1 - y, k, y_sem, partner).wait_recv()

        @pl.when(s == 0)
        def _():
            load(k).wait()

        part = nt(gath[k, pl.ds(pl.multiple_of(p * 64, 64), 64), :], st[k])

        @pl.when(k == 0)
        def _():
            acc[...] = part

        @pl.when(k > 0)
        def _():
            acc[...] += part

        @pl.when((k == N_CHUNK - 1) & (p == mine))
        def _():
            out_ref[...] = acc[...]

        @pl.when((k == N_CHUNK - 1) & (p != mine))
        def _():
            sbuf[s] = acc[...].astype(bf16)
            hand_over(p, s).start()

    steps = nz * N_CHUNK

    def first(t, carry):
        forward(t)
        return carry

    def body(t, carry):
        @pl.when(t + N_CHUNK < steps)
        def _():
            forward(t + N_CHUNK)

        compute(t)
        return carry

    lax.fori_loop(0, N_CHUNK, first, 0)
    lax.fori_loop(0, steps, body, 0)

    def drain(t, carry):
        p, k = t // N_CHUNK, t % N_CHUNK

        @pl.when((p <= z) & (z < nz - 1))
        def _():
            send(p, y, k, up_sem, me + 2).wait_send()

        @pl.when((p >= z) & (z > 0))
        def _():
            send(p, y, k, down_sem, me - 2).wait_send()

        send(p, y, k, y_sem, partner).wait_send()
        return carry

    lax.fori_loop(0, steps, drain, 0)

    total = out_ref[...]
    for step in range(1, layers):
        other = lax.rem(mine + step, layers)
        pltpu.make_async_remote_copy(
            src_ref=sbuf.at[0], dst_ref=rbuf.at[other], send_sem=rs_send.at[0],
            recv_sem=rs_recv.at[other], device_id={"layer": other}, device_id_type=MESH,
        ).wait_recv()
        total = total + rbuf[other].astype(f32)
    live = iota(total.shape, 1) < cnt_ref[0]
    out_ref[...] = jnp.where(live, total, 0.0)
    for s in range(nz):
        p = plane_at(s)

        @pl.when(p != mine)
        def _():
            hand_over(p, s).wait_send()


def in_one_kernel(nz, query_grads, stored_grads, basis_in, basis_out, eigen_values, layer_mask, doc_counts):
    layers = nz
    _, docs, depth = stored_grads.shape
    queries = layer_mask.shape[0]
    rows = queries // layers
    width = depth // N_CHUNK
    vmem = pl.BlockSpec(memory_space=pltpu.VMEM)
    return pl.pallas_call(
        functools.partial(kernel, nz),
        out_shape=jax.ShapeDtypeStruct((rows, docs), f32),
        in_specs=[vmem, pl.BlockSpec(memory_space=pl.ANY), vmem, vmem, vmem, vmem,
                  pl.BlockSpec(memory_space=pltpu.SMEM)],
        out_specs=vmem,
        scratch_shapes=[
            pltpu.VMEM((N_CHUNK, docs, width), bf16),
            pltpu.VMEM((N_CHUNK, queries, width), bf16),
            pltpu.VMEM((rows, docs), f32),
            pltpu.VMEM((layers, rows, docs), bf16),
            pltpu.VMEM((layers, rows, docs), bf16),
            pltpu.SemaphoreType.DMA((N_CHUNK,)),
            pltpu.SemaphoreType.DMA((2 * nz, N_CHUNK)),
            pltpu.SemaphoreType.DMA((nz, N_CHUNK)),
            pltpu.SemaphoreType.DMA((nz, N_CHUNK)),
            pltpu.SemaphoreType.DMA((nz, N_CHUNK)),
            pltpu.SemaphoreType.DMA((layers,)),
            pltpu.SemaphoreType.DMA((layers,)),
        ],
        compiler_params=pltpu.CompilerParams(
            collective_id=0, has_side_effects=True, vmem_limit_bytes=58 * 1024 * 1024
        ),
        cost_estimate=pl.CostEstimate(
            flops=2 * queries * docs * depth, bytes_accessed=2 * docs * depth, transcendentals=0
        ),
    )(query_grads, stored_grads, basis_in, basis_out, eigen_values, layer_mask, doc_counts)


def on_device(query_grads, stored_grads, *rest):
    n_doc, layers = lax.axis_size("doc"), lax.axis_size("layer")
    shape = query_grads.shape
    if n_doc == 8 and layers == 4 and shape == (1, 32, 4096):
        return in_one_kernel(n_doc // 2, query_grads, stored_grads, *rest)
    return by_collectives(query_grads, stored_grads, *rest)


def solution(mesh):
    in_specs = (
        P("layer", "doc", None),
        P("layer", "doc", None),
        P("layer", None, None),
        P("layer", None, None),
        P("layer", None, None),
        P(None, "layer"),
        P("doc"),
    )
    out_specs = P("layer", "doc")
    return jax.shard_map(
        on_device, mesh=mesh, in_specs=in_specs, out_specs=out_specs, check_vma=False
    )
```

```python
import functools
import jax
import jax.numpy as jnp
from jax import lax
from jax.experimental import pallas as pl
from jax.experimental.pallas import tpu as pltpu
from jax.sharding import PartitionSpec as P

damping = 0.1
N_CHUNK = 4
MESH = pl.DeviceIdType.MESH
f32 = jnp.float32
bf16 = jnp.bfloat16


def precondition(gradients, basis_in, basis_out, eigen_values):
    row_count = gradients.shape[0]
    grid_blocks = gradients.astype(jnp.float32).reshape(
        row_count, basis_out.shape[0], basis_in.shape[0]
    )
    rotated = jnp.einsum(
        "xi,qxy,yj->qij", basis_out, grid_blocks, basis_in, precision=lax.Precision.HIGHEST
    )
    scaled = rotated / (eigen_values + damping)
    restored = jnp.einsum(
        "bi,qij,aj->qba", basis_out, scaled, basis_in, precision=lax.Precision.HIGHEST
    )
    return restored.reshape(row_count, -1).astype(jnp.bfloat16)


def by_collectives(query_grads, stored_grads, basis_in, basis_out, eigen_values, layer_mask, doc_counts):
    stored = stored_grads[0]
    row_weights = layer_mask[:, 0].astype(jnp.bfloat16)
    own_rows = precondition(query_grads[0], basis_in[0], basis_out[0], eigen_values[0])
    masked = lax.all_gather(own_rows, "doc", axis=0, tiled=True) * row_weights[:, None]
    score_tiles = lax.dot_general(
        masked, stored, (((1,), (1,)), ((), ())), preferred_element_type=jnp.float32
    )
    live_slots = jnp.arange(stored.shape[0], dtype=jnp.int32) < doc_counts[0]
    score_tiles = jnp.where(live_slots[None, :], score_tiles, jnp.zeros_like(score_tiles))
    return lax.psum_scatter(score_tiles, "layer", scatter_dimension=0, tiled=True)


def halves(x):
    hi = x.astype(bf16)
    return hi, (x - hi.astype(f32)).astype(bf16)


def nn(a, b):
    return lax.dot_general(a, b, (((1,), (0,)), ((), ())), preferred_element_type=f32)


def nt(a, b):
    return lax.dot_general(a, b, (((1,), (1,)), ((), ())), preferred_element_type=f32)


def one_hot(hits):
    return jnp.where(hits, 1.0, 0.0).astype(bf16)


def iota(shape, dim):
    return lax.broadcasted_iota(jnp.int32, shape, dim)


def write_own_rows(q_ref, bi_ref, bo_ref, ev_ref, mask_ref, gath, me):
    x = q_ref[0].astype(f32)
    r, c = iota((256, 256), 0), iota((256, 256), 1)
    same = (r // 128 == (c // 64) % 2) & ((r // 64) % 2 == c // 128)
    put_a = one_hot(iota((256, 64), 0) % 64 == iota((256, 64), 1))
    wa = [
        jnp.where(same, nt(nn(put_a, part).astype(bf16), put_a), 0.0).astype(bf16)
        for part in halves(bi_ref[0])
    ]
    row = iota((512, 64), 0)
    put_b = one_hot(2 * ((row // 8) % 32) + row // 256 == iota((512, 64), 1))
    eye = iota((512, 512), 0) % 8 == iota((512, 512), 1) % 8
    wc, wb = [], []
    for part in halves(bo_ref[0]):
        wc.append(jnp.where(eye, nt(nn(put_b, part).astype(bf16), put_b), 0.0).astype(bf16))
        wb.append(jnp.where(eye, nt(nt(put_b, part).astype(bf16), put_b), 0.0).astype(bf16))
    inverse = 1.0 / (ev_ref[0] + damping)
    top, low = halves(inverse)
    low = inverse - top.astype(f32)
    mid, low = halves(low)
    scale = 0.0
    for part in (top, mid, low):
        scale = scale + nt(nn(put_b, part).astype(bf16), put_a)

    turned = []
    for gp in range(2):
        pieces = [
            jnp.concatenate(
                [
                    x[8 * (2 * gp + g) : 8 * (2 * gp + g) + 8, 128 * j : 128 * j + 128]
                    for j in range(32)
                ],
                axis=0,
            )
            for g in range(2)
        ]
        block = jnp.concatenate(pieces, axis=1).astype(bf16)
        turned.append(nn(block, wa[0]) + nn(block, wa[1]))
    s = jnp.concatenate(
        [
            jnp.concatenate([turned[gp][:, 128 * p : 128 * p + 128] for gp in range(2)], axis=1)
            for p in range(2)
        ],
        axis=0,
    )
    s_hi, s_lo = halves(s)
    rotated = nn(wb[0], s_hi) + (nn(wb[0], s_lo) + nn(wb[1], s_hi))
    v_hi, v_lo = halves(rotated * scale)
    v = nn(wc[0], v_hi) + (nn(wc[0], v_lo) + nn(wc[1], v_hi))
    picked = iota((32, 256), 1) == me * 32 + iota((32, 256), 0)
    weights = jnp.sum(jnp.where(picked, mask_ref[...].astype(f32), 0.0), axis=1, keepdims=True)
    for gp in range(2):
        y = jnp.concatenate(
            [v[256 * p : 256 * p + 256, 128 * gp : 128 * gp + 128] for p in range(2)], axis=1
        )
        y_hi, y_lo = halves(y)
        done = nt(y_hi, wa[0]) + (nt(y_lo, wa[0]) + nt(y_hi, wa[1]))
        w16 = weights[16 * gp : 16 * gp + 16, :]
        rows = pl.ds(pl.multiple_of(me * 32 + 16 * gp, 16), 16)
        for j in range(32):
            tile = jnp.concatenate(
                [done[8 * j : 8 * j + 8, :128], done[8 * j : 8 * j + 8, 128:]], axis=0
            )
            gath[j // 8, rows, 128 * (j % 8) : 128 * (j % 8) + 128] = (tile * w16).astype(bf16)


def kernel(
    nz, q_ref, stored_ref, bi_ref, bo_ref, ev_ref, mask_ref, out_ref,
    st, gath, acc, sbuf, rbuf,
    st_sem, recv_sem, up_sem, down_sem, y_sem, rs_send, rs_recv,
):
    layers = sbuf.shape[0]
    width = st.shape[2]
    parts = sbuf.shape[1]
    me = lax.axis_index("doc")
    mine = lax.axis_index("layer")
    z, y = me // 2, me % 2
    partner = me + 1 - 2 * y

    def load(k):
        return pltpu.make_async_copy(
            stored_ref.at[0, :, pl.ds(k * width, width)], st.at[k], st_sem.at[k]
        )

    for k in range(N_CHUNK):
        load(k).start()

    barrier = pltpu.get_barrier_semaphore()
    pl.semaphore_signal(barrier, inc=1, device_id={"doc": partner}, device_id_type=MESH)
    for step in range(1, layers):
        pl.semaphore_signal(
            barrier, inc=1, device_id={"layer": lax.rem(mine + step, layers)}, device_id_type=MESH
        )

    @pl.when(z < nz - 1)
    def _():
        pl.semaphore_signal(barrier, inc=1, device_id={"doc": me + 2}, device_id_type=MESH)

    @pl.when(z > 0)
    def _():
        pl.semaphore_signal(barrier, inc=1, device_id={"doc": me - 2}, device_id_type=MESH)

    write_own_rows(q_ref, bi_ref, bo_ref, ev_ref, mask_ref, gath, me)

    ends = jnp.where(z == 0, 1, 0) + jnp.where(z == nz - 1, 1, 0)
    pl.semaphore_wait(barrier, layers + 2 - ends)

    def plane_at(s):
        far = (z >= 2).astype(jnp.int32)
        near = z + far * (3 - 2 * z)
        inner = (near == 1).astype(jnp.int32)
        swap = inner * jnp.where(s < 2, 1, 0)
        p = s + swap * (1 - 2 * s)
        return p + far * (3 - 2 * p)

    def send(p, side, k, sems, target):
        blk = 2 * p + side
        part = gath.at[k, pl.ds(pl.multiple_of(blk * 32, 32), 32)]
        return pltpu.make_async_remote_copy(
            src_ref=part, dst_ref=part, send_sem=sems.at[blk, k], recv_sem=recv_sem.at[blk, k],
            device_id={"doc": target}, device_id_type=MESH,
        )

    def up(p, side, k):
        return send(p, side, k, up_sem, me + 2)

    def down(p, side, k):
        return send(p, side, k, down_sem, me - 2)

    def across(p, k):
        return send(p, y, k, y_sem, partner)

    def landed(p, side, k):
        return send(p, side, k, y_sem, partner)

    def both_columns(p, k):
        return ((p == 0) | (p == nz - 1)) & (k % 2 == 1)

    def goes_up(p):
        return (p <= z) & (z < nz - 1)

    def goes_down(p):
        return (p >= z) & (z > 0)

    def goes_across(p, k):
        return (p == z) | jnp.logical_not(both_columns(p, k))

    def relayed(p, k):
        return both_columns(p, k) & (p != z) & (p + z != nz - 1)

    def forward(t):
        p, k = plane_at(t // N_CHUNK), t % N_CHUNK

        @pl.when(p != z)
        def _():
            landed(p, y, k).wait_recv()

        @pl.when(goes_up(p))
        def _():
            up(p, y, k).start()

        @pl.when(goes_down(p))
        def _():
            down(p, y, k).start()

        @pl.when(goes_across(p, k))
        def _():
            across(p, k).start()

    def pass_on(p, k):
        @pl.when(goes_up(p))
        def _():
            up(p, 1 - y, k).start()

        @pl.when(goes_down(p))
        def _():
            down(p, 1 - y, k).start()

    def relay(t):
        p, k = plane_at(t // N_CHUNK), t % N_CHUNK

        @pl.when(relayed(p, k))
        def _():
            landed(p, 1 - y, k).wait_recv()
            pass_on(p, k)

    def hand_over(p, s, n):
        return pltpu.make_async_remote_copy(
            src_ref=sbuf.at[s, n], dst_ref=rbuf.at[mine, n], send_sem=rs_send.at[s, n],
            recv_sem=rs_recv.at[mine, n], device_id={"layer": p}, device_id_type=MESH,
        )

    def compute(t):
        s, k = t // N_CHUNK, t % N_CHUNK
        p = plane_at(s)

        @pl.when(jnp.logical_not(relayed(p, k)))
        def _():
            landed(p, 1 - y, k).wait_recv()

        @pl.when((s == 0) & both_columns(p, k))
        def _():
            pass_on(p, k)

        @pl.when(s == 0)
        def _():
            load(k).wait()

        rows = pl.ds(pl.multiple_of(p * 64, 64), 64)

        @pl.when(k == 0)
        def _():
            acc[...] = nt(gath[k, rows, :], st[k])

        @pl.when((k > 0) & (k < N_CHUNK - 1))
        def _():
            acc[...] += nt(gath[k, rows, :], st[k])

        @pl.when(k == N_CHUNK - 1)
        def _():
            def column(n, carry):
                cols = pl.ds(pl.multiple_of(n * 256, 256), 256)
                total = acc[:, cols] + nt(gath[k, rows, :], st[k, cols, :])

                @pl.when(p == mine)
                def _():
                    out_ref[:, cols] = total

                @pl.when(p != mine)
                def _():
                    sbuf[s, n] = total.astype(bf16)
                    hand_over(p, s, n).start()

                return carry

            lax.fori_loop(0, parts, column, 0)

    steps = nz * N_CHUNK

    def first(t, carry):
        forward(t)
        return carry

    def body(t, carry):
        @pl.when(t + N_CHUNK < steps)
        def _():
            forward(t + N_CHUNK)

        @pl.when(t + 1 < steps)
        def _():
            relay(t + 1)

        compute(t)
        return carry

    lax.fori_loop(0, N_CHUNK, first, 0)
    lax.fori_loop(0, steps, body, 0)

    def collect(n, carry):
        cols = pl.ds(pl.multiple_of(n * 256, 256), 256)
        total = out_ref[:, cols]
        for step in range(1, layers):
            other = lax.rem(mine + step, layers)
            pltpu.make_async_remote_copy(
                src_ref=sbuf.at[0, n], dst_ref=rbuf.at[other, n], send_sem=rs_send.at[0, n],
                recv_sem=rs_recv.at[other, n], device_id={"layer": other}, device_id_type=MESH,
            ).wait_recv()
            total = total + rbuf[other, n].astype(f32)
        out_ref[:, cols] = total
        return carry

    lax.fori_loop(0, parts, collect, 0)

    def drain(t, carry):
        p, k = t // N_CHUNK, t % N_CHUNK

        @pl.when(goes_up(p))
        def _():
            up(p, y, k).wait_send()

        @pl.when(goes_down(p))
        def _():
            down(p, y, k).wait_send()

        @pl.when(both_columns(p, k) & goes_up(p))
        def _():
            up(p, 1 - y, k).wait_send()

        @pl.when(both_columns(p, k) & goes_down(p))
        def _():
            down(p, 1 - y, k).wait_send()

        @pl.when(goes_across(p, k))
        def _():
            across(p, k).wait_send()

        return carry

    lax.fori_loop(0, steps, drain, 0)

    def drain_scores(t, carry):
        s, n = t // parts, t % parts
        p = plane_at(s)

        @pl.when(p != mine)
        def _():
            hand_over(p, s, n).wait_send()

        return carry

    lax.fori_loop(0, nz * parts, drain_scores, 0)


def in_one_kernel(nz, query_grads, stored_grads, basis_in, basis_out, eigen_values, layer_mask, doc_counts):
    layers = nz
    _, docs, depth = stored_grads.shape
    queries = layer_mask.shape[0]
    rows = queries // layers
    width = depth // N_CHUNK
    vmem = pl.BlockSpec(memory_space=pltpu.VMEM)
    summed = pl.pallas_call(
        functools.partial(kernel, nz),
        out_shape=jax.ShapeDtypeStruct((rows, docs), f32),
        in_specs=[vmem, pl.BlockSpec(memory_space=pl.ANY), vmem, vmem, vmem, vmem],
        out_specs=vmem,
        scratch_shapes=[
            pltpu.VMEM((N_CHUNK, docs, width), bf16),
            pltpu.VMEM((N_CHUNK, queries, width), bf16),
            pltpu.VMEM((rows, docs), f32),
            pltpu.VMEM((nz, docs // 256, rows, 256), bf16),
            pltpu.VMEM((layers, docs // 256, rows, 256), bf16),
            pltpu.SemaphoreType.DMA((N_CHUNK,)),
            pltpu.SemaphoreType.DMA((2 * nz, N_CHUNK)),
            pltpu.SemaphoreType.DMA((2 * nz, N_CHUNK)),
            pltpu.SemaphoreType.DMA((2 * nz, N_CHUNK)),
            pltpu.SemaphoreType.DMA((2 * nz, N_CHUNK)),
            pltpu.SemaphoreType.DMA((nz, docs // 256)),
            pltpu.SemaphoreType.DMA((layers, docs // 256)),
        ],
        compiler_params=pltpu.CompilerParams(
            collective_id=0, has_side_effects=True, vmem_limit_bytes=58 * 1024 * 1024
        ),
        cost_estimate=pl.CostEstimate(
            flops=2 * queries * docs * depth, bytes_accessed=2 * docs * depth, transcendentals=0
        ),
    )(query_grads, stored_grads, basis_in, basis_out, eigen_values, layer_mask.reshape(1, queries))
    live_slots = jnp.arange(docs, dtype=jnp.int32) < doc_counts[0]
    return jnp.where(live_slots[None, :], summed, jnp.zeros_like(summed))


def on_device(query_grads, stored_grads, *rest):
    n_doc, layers = lax.axis_size("doc"), lax.axis_size("layer")
    shape = query_grads.shape
    if n_doc == 8 and layers == 4 and shape == (1, 32, 4096):
        return in_one_kernel(n_doc // 2, query_grads, stored_grads, *rest)
    return by_collectives(query_grads, stored_grads, *rest)


def solution(mesh):
    in_specs = (
        P("layer", "doc", None),
        P("layer", "doc", None),
        P("layer", None, None),
        P("layer", None, None),
        P("layer", None, None),
        P(None, "layer"),
        P("doc"),
    )
    out_specs = P("layer", "doc")
    return jax.shard_map(
        on_device, mesh=mesh, in_specs=in_specs, out_specs=out_specs, check_vma=False
    )
```

```python
import functools
import jax
import jax.numpy as jnp
from jax import lax
from jax.experimental import pallas as pl
from jax.experimental.pallas import tpu as pltpu
from jax.sharding import PartitionSpec as P

damping = 0.1
N_CHUNK = 4
MESH = pl.DeviceIdType.MESH
f32 = jnp.float32
bf16 = jnp.bfloat16


def precondition(gradients, basis_in, basis_out, eigen_values):
    row_count = gradients.shape[0]
    grid_blocks = gradients.astype(jnp.float32).reshape(
        row_count, basis_out.shape[0], basis_in.shape[0]
    )
    rotated = jnp.einsum(
        "xi,qxy,yj->qij", basis_out, grid_blocks, basis_in, precision=lax.Precision.HIGHEST
    )
    scaled = rotated / (eigen_values + damping)
    restored = jnp.einsum(
        "bi,qij,aj->qba", basis_out, scaled, basis_in, precision=lax.Precision.HIGHEST
    )
    return restored.reshape(row_count, -1).astype(jnp.bfloat16)


def by_collectives(query_grads, stored_grads, basis_in, basis_out, eigen_values, layer_mask, doc_counts):
    stored = stored_grads[0]
    row_weights = layer_mask[:, 0].astype(jnp.bfloat16)
    own_rows = precondition(query_grads[0], basis_in[0], basis_out[0], eigen_values[0])
    masked = lax.all_gather(own_rows, "doc", axis=0, tiled=True) * row_weights[:, None]
    score_tiles = lax.dot_general(
        masked, stored, (((1,), (1,)), ((), ())), preferred_element_type=jnp.float32
    )
    live_slots = jnp.arange(stored.shape[0], dtype=jnp.int32) < doc_counts[0]
    score_tiles = jnp.where(live_slots[None, :], score_tiles, jnp.zeros_like(score_tiles))
    return lax.psum_scatter(score_tiles, "layer", scatter_dimension=0, tiled=True)


def halves(x):
    hi = x.astype(bf16)
    return hi, (x - hi.astype(f32)).astype(bf16)


def nn(a, b):
    return lax.dot_general(a, b, (((1,), (0,)), ((), ())), preferred_element_type=f32)


def nt(a, b):
    return lax.dot_general(a, b, (((1,), (1,)), ((), ())), preferred_element_type=f32)


def three(a, b_hi, b_lo):
    both = nn(a[0], jnp.concatenate([b_hi, b_lo], axis=1))
    width = b_hi.shape[1]
    return both[:, :width] + (both[:, width:] + nn(a[1], b_hi))


def one_hot(hits):
    return jnp.where(hits, 1.0, 0.0).astype(bf16)


def iota(shape, dim):
    return lax.broadcasted_iota(jnp.int32, shape, dim)


def write_own_rows(q_ref, bi_ref, bo_ref, ev_ref, mask_ref, gath, me, ready, send_rows):
    r, c = iota((256, 256), 0), iota((256, 256), 1)
    same = (r // 128 == (c // 64) % 2) & ((r // 64) % 2 == c // 128)
    put_a = one_hot(iota((256, 64), 0) % 64 == iota((256, 64), 1))
    wa = [
        jnp.where(same, nt(nn(put_a, part).astype(bf16), put_a), 0.0).astype(bf16)
        for part in halves(bi_ref[0])
    ]
    row = iota((512, 64), 0)
    put_b = one_hot(2 * ((row // 8) % 32) + row // 256 == iota((512, 64), 1))
    eye = iota((512, 512), 0) % 8 == iota((512, 512), 1) % 8
    wc, wb = [], []
    for part in halves(bo_ref[0]):
        wc.append(jnp.where(eye, nt(nn(put_b, part).astype(bf16), put_b), 0.0).astype(bf16))
        wb.append(jnp.where(eye, nt(nt(put_b, part).astype(bf16), put_b), 0.0).astype(bf16))
    inverse = 1.0 / (ev_ref[0] + damping)
    top, low = halves(inverse)
    low = inverse - top.astype(f32)
    mid, low = halves(low)
    scale = 0.0
    for part in (top, mid, low):
        scale = scale + nt(nn(put_b, part).astype(bf16), put_a[:128])
    ready()


    def rows_of_16(gp, carry):
        x = q_ref[0, pl.ds(pl.multiple_of(16 * gp, 16), 16), :].astype(f32)
        block = jnp.concatenate(
            [
                jnp.concatenate(
                    [x[8 * g : 8 * g + 8, 128 * j : 128 * j + 128] for j in range(32)], axis=0
                )
                for g in range(2)
            ],
            axis=1,
        ).astype(bf16)
        turned = nn(block, wa[0]) + nn(block, wa[1])
        s = jnp.concatenate([turned[:, :128], turned[:, 128:]], axis=0)
        s_hi, s_lo = halves(s)
        rotated = three(wb, s_hi, s_lo)
        v_hi, v_lo = halves(rotated * scale)
        v = three(wc, v_hi, v_lo)
        y_hi, y_lo = halves(jnp.concatenate([v[:256], v[256:]], axis=1))
        done = nt(y_hi, wa[0]) + (nt(y_lo, wa[0]) + nt(y_hi, wa[1]))
        start = me * 32 + 16 * gp
        picked = iota((16, 256), 1) == start + iota((16, 256), 0)
        w16 = jnp.sum(jnp.where(picked, mask_ref[...].astype(f32), 0.0), axis=1, keepdims=True)
        rows = pl.ds(pl.multiple_of(start, 16), 16)
        for j in range(32):
            tile = jnp.concatenate(
                [done[8 * j : 8 * j + 8, :128], done[8 * j : 8 * j + 8, 128:]], axis=0
            )
            gath[j // 8, rows, 128 * (j % 8) : 128 * (j % 8) + 128] = (tile * w16).astype(bf16)
        send_rows(gp)
        return carry

    lax.fori_loop(0, 2, rows_of_16, 0)


def kernel(
    nz, q_ref, stored_ref, bi_ref, bo_ref, ev_ref, mask_ref, out_ref,
    st, gath, acc, sbuf, rbuf,
    st_sem, recv_sem, up_sem, down_sem, y_sem, rs_send, rs_recv,
):
    layers = sbuf.shape[0]
    width = st.shape[2]
    parts = sbuf.shape[1]
    me = lax.axis_index("doc")
    mine = lax.axis_index("layer")
    z, y = me // 2, me % 2
    partner = me + 1 - 2 * y

    def load(k):
        return pltpu.make_async_copy(
            stored_ref.at[0, :, pl.ds(k * width, width)], st.at[k], st_sem.at[k]
        )

    for k in range(N_CHUNK):
        load(k).start()

    barrier = pltpu.get_barrier_semaphore()
    pl.semaphore_signal(barrier, inc=1, device_id={"doc": partner}, device_id_type=MESH)
    for step in range(1, layers):
        pl.semaphore_signal(
            barrier, inc=1, device_id={"layer": lax.rem(mine + step, layers)}, device_id_type=MESH
        )

    @pl.when(z < nz - 1)
    def _():
        pl.semaphore_signal(barrier, inc=1, device_id={"doc": me + 2}, device_id_type=MESH)

    @pl.when(z > 0)
    def _():
        pl.semaphore_signal(barrier, inc=1, device_id={"doc": me - 2}, device_id_type=MESH)

    def plane_at(s):
        far = (z >= 2).astype(jnp.int32)
        near = z + far * (3 - 2 * z)
        inner = (near == 1).astype(jnp.int32)
        swap = inner * jnp.where(s < 2, 1, 0)
        p = s + swap * (1 - 2 * s)
        return p + far * (3 - 2 * p)

    def send(p, side, k, sems, target, gp=None):
        blk = 2 * p + side
        if gp is None:
            part = gath.at[k, pl.ds(pl.multiple_of(blk * 32, 32), 32)]
        else:
            part = gath.at[k, pl.ds(pl.multiple_of(blk * 32 + gp * 16, 16), 16)]
        return pltpu.make_async_remote_copy(
            src_ref=part, dst_ref=part, send_sem=sems.at[blk, k], recv_sem=recv_sem.at[blk, k],
            device_id={"doc": target}, device_id_type=MESH,
        )

    def up(p, side, k, gp=None):
        return send(p, side, k, up_sem, me + 2, gp)

    def down(p, side, k, gp=None):
        return send(p, side, k, down_sem, me - 2, gp)

    def across(p, k, gp=None):
        return send(p, y, k, y_sem, partner, gp)

    def landed(p, side, k):
        return send(p, side, k, y_sem, partner)

    def both_columns(p, k):
        return ((p == 0) | (p == nz - 1)) & (k % 2 == 1)

    def goes_up(p):
        return (p <= z) & (z < nz - 1)

    def goes_down(p):
        return (p >= z) & (z > 0)

    def goes_across(p, k):
        return (p == z) | jnp.logical_not(both_columns(p, k))

    def relayed(p, k):
        return both_columns(p, k) & (p != z) & (p + z != nz - 1)

    def forward(t):
        p, k = plane_at(t // N_CHUNK), t % N_CHUNK

        landed(p, y, k).wait_recv()

        @pl.when(goes_up(p))
        def _():
            up(p, y, k).start()

        @pl.when(goes_down(p))
        def _():
            down(p, y, k).start()

        @pl.when(jnp.logical_not(both_columns(p, k)))
        def _():
            across(p, k).start()

    def send_rows(gp):
        def chunk(k, carry):
            @pl.when(z < nz - 1)
            def _():
                up(z, y, k, gp).start()

            @pl.when(z > 0)
            def _():
                down(z, y, k, gp).start()

            across(z, k, gp).start()
            return carry

        lax.fori_loop(0, N_CHUNK, chunk, 0)

    def ready():
        ends = jnp.where(z == 0, 1, 0) + jnp.where(z == nz - 1, 1, 0)
        pl.semaphore_wait(barrier, layers + 2 - ends)

    def pass_on(p, k):
        @pl.when(goes_up(p))
        def _():
            up(p, 1 - y, k).start()

        @pl.when(goes_down(p))
        def _():
            down(p, 1 - y, k).start()

    def relay(t):
        p, k = plane_at(t // N_CHUNK), t % N_CHUNK

        @pl.when(relayed(p, k))
        def _():
            landed(p, 1 - y, k).wait_recv()
            pass_on(p, k)

    def hand_over(p, s, n):
        return pltpu.make_async_remote_copy(
            src_ref=sbuf.at[s, n], dst_ref=rbuf.at[mine, n], send_sem=rs_send.at[s, n],
            recv_sem=rs_recv.at[mine, n], device_id={"layer": p}, device_id_type=MESH,
        )

    def compute(t):
        s, k = t // N_CHUNK, t % N_CHUNK
        p = plane_at(s)

        @pl.when(jnp.logical_not(relayed(p, k)))
        def _():
            landed(p, 1 - y, k).wait_recv()

        @pl.when((s == 0) & both_columns(p, k))
        def _():
            pass_on(p, k)

        @pl.when(s == 0)
        def _():
            load(k).wait()

        rows = pl.ds(pl.multiple_of(p * 64, 64), 64)

        @pl.when(k == 0)
        def _():
            acc[...] = jnp.zeros_like(acc)

        @pl.when(k < N_CHUNK - 1)
        def _():
            acc[...] += nt(gath[k, rows, :], st[k])

        @pl.when(k == N_CHUNK - 1)
        def _():
            def column(n, carry):
                cols = pl.ds(pl.multiple_of(n * 256, 256), 256)
                total = acc[:, cols] + nt(gath[k, rows, :], st[k, cols, :])

                @pl.when(p == mine)
                def _():
                    out_ref[:, cols] = total

                @pl.when(p != mine)
                def _():
                    sbuf[s, n] = total.astype(bf16)
                    hand_over(p, s, n).start()

                return carry

            lax.fori_loop(0, parts, column, 0)

    steps = nz * N_CHUNK

    def first(t, carry):
        forward(t)
        return carry

    def body(t, carry):
        @pl.when(t + lead < steps)
        def _():
            forward(t + lead)

        @pl.when(t + 2 < steps)
        def _():
            relay(t + 2)

        compute(t)
        return carry

    write_own_rows(q_ref, bi_ref, bo_ref, ev_ref, mask_ref, gath, me, ready, send_rows)
    lead = N_CHUNK * jnp.where((z == 0) | (z == nz - 1), 1, 2)
    lax.fori_loop(N_CHUNK, lead, first, 0)
    lax.fori_loop(0, steps, body, 0)

    def collect(n, carry):
        cols = pl.ds(pl.multiple_of(n * 256, 256), 256)
        total = out_ref[:, cols]
        for step in range(1, layers):
            other = lax.rem(mine + step, layers)
            pltpu.make_async_remote_copy(
                src_ref=sbuf.at[0, n], dst_ref=rbuf.at[other, n], send_sem=rs_send.at[0, n],
                recv_sem=rs_recv.at[other, n], device_id={"layer": other}, device_id_type=MESH,
            ).wait_recv()
            total = total + rbuf[other, n].astype(f32)
        out_ref[:, cols] = total
        return carry

    lax.fori_loop(0, parts, collect, 0)

    def drain(t, carry):
        p, k = t // N_CHUNK, t % N_CHUNK

        @pl.when(goes_up(p))
        def _():
            up(p, y, k).wait_send()

        @pl.when(goes_down(p))
        def _():
            down(p, y, k).wait_send()

        @pl.when(both_columns(p, k) & goes_up(p))
        def _():
            up(p, 1 - y, k).wait_send()

        @pl.when(both_columns(p, k) & goes_down(p))
        def _():
            down(p, 1 - y, k).wait_send()

        @pl.when(goes_across(p, k))
        def _():
            across(p, k).wait_send()

        return carry

    lax.fori_loop(0, steps, drain, 0)

    def drain_scores(t, carry):
        s, n = t // parts, t % parts
        p = plane_at(s)

        @pl.when(p != mine)
        def _():
            hand_over(p, s, n).wait_send()

        return carry

    lax.fori_loop(0, nz * parts, drain_scores, 0)


def in_one_kernel(nz, query_grads, stored_grads, basis_in, basis_out, eigen_values, layer_mask, doc_counts):
    layers = nz
    _, docs, depth = stored_grads.shape
    queries = layer_mask.shape[0]
    rows = queries // layers
    width = depth // N_CHUNK
    vmem = pl.BlockSpec(memory_space=pltpu.VMEM)
    summed = pl.pallas_call(
        functools.partial(kernel, nz),
        out_shape=jax.ShapeDtypeStruct((rows, docs), f32),
        in_specs=[vmem, pl.BlockSpec(memory_space=pltpu.HBM), vmem, vmem, vmem, vmem],
        out_specs=vmem,
        scratch_shapes=[
            pltpu.VMEM((N_CHUNK, docs, width), bf16),
            pltpu.VMEM((N_CHUNK, queries, width), bf16),
            pltpu.VMEM((rows, docs), f32),
            pltpu.VMEM((nz, docs // 256, rows, 256), bf16),
            pltpu.VMEM((layers, docs // 256, rows, 256), bf16),
            pltpu.SemaphoreType.DMA((N_CHUNK,)),
            pltpu.SemaphoreType.DMA((2 * nz, N_CHUNK)),
            pltpu.SemaphoreType.DMA((2 * nz, N_CHUNK)),
            pltpu.SemaphoreType.DMA((2 * nz, N_CHUNK)),
            pltpu.SemaphoreType.DMA((2 * nz, N_CHUNK)),
            pltpu.SemaphoreType.DMA((nz, docs // 256)),
            pltpu.SemaphoreType.DMA((layers, docs // 256)),
        ],
        compiler_params=pltpu.CompilerParams(
            collective_id=0, has_side_effects=True, vmem_limit_bytes=50 * 1024 * 1024
        ),
        cost_estimate=pl.CostEstimate(
            flops=2 * queries * docs * depth, bytes_accessed=2 * docs * depth, transcendentals=0
        ),
    )(query_grads, stored_grads, basis_in, basis_out, eigen_values, layer_mask.reshape(1, queries))
    live_slots = jnp.arange(docs, dtype=jnp.int32) < doc_counts[0]
    return jnp.where(live_slots[None, :], summed, jnp.zeros_like(summed))


def on_device(query_grads, stored_grads, *rest):
    n_doc, layers = lax.axis_size("doc"), lax.axis_size("layer")
    shape = query_grads.shape
    if n_doc == 8 and layers == 4 and shape == (1, 32, 4096):
        return in_one_kernel(n_doc // 2, query_grads, stored_grads, *rest)
    return by_collectives(query_grads, stored_grads, *rest)


def solution(mesh):
    in_specs = (
        P("layer", "doc", None),
        P("layer", "doc", None),
        P("layer", None, None),
        P("layer", None, None),
        P("layer", None, None),
        P(None, "layer"),
        P("doc"),
    )
    out_specs = P("layer", "doc")
    return jax.shard_map(
        on_device, mesh=mesh, in_specs=in_specs, out_specs=out_specs, check_vma=False
    )
```

```python
import functools
import jax
import jax.numpy as jnp
from jax import lax
from jax.experimental import pallas as pl
from jax.experimental.pallas import tpu as pltpu
from jax.sharding import PartitionSpec as P

damping = 0.1
N_CHUNK = 4
MESH = pl.DeviceIdType.MESH
f32 = jnp.float32
bf16 = jnp.bfloat16


def precondition(gradients, basis_in, basis_out, eigen_values):
    row_count = gradients.shape[0]
    grid_blocks = gradients.astype(jnp.float32).reshape(
        row_count, basis_out.shape[0], basis_in.shape[0]
    )
    rotated = jnp.einsum(
        "xi,qxy,yj->qij", basis_out, grid_blocks, basis_in, precision=lax.Precision.HIGHEST
    )
    scaled = rotated / (eigen_values + damping)
    restored = jnp.einsum(
        "bi,qij,aj->qba", basis_out, scaled, basis_in, precision=lax.Precision.HIGHEST
    )
    return restored.reshape(row_count, -1).astype(jnp.bfloat16)


def by_collectives(query_grads, stored_grads, basis_in, basis_out, eigen_values, layer_mask, doc_counts):
    stored = stored_grads[0]
    row_weights = layer_mask[:, 0].astype(jnp.bfloat16)
    own_rows = precondition(query_grads[0], basis_in[0], basis_out[0], eigen_values[0])
    masked = lax.all_gather(own_rows, "doc", axis=0, tiled=True) * row_weights[:, None]
    score_tiles = lax.dot_general(
        masked, stored, (((1,), (1,)), ((), ())), preferred_element_type=jnp.float32
    )
    live_slots = jnp.arange(stored.shape[0], dtype=jnp.int32) < doc_counts[0]
    score_tiles = jnp.where(live_slots[None, :], score_tiles, jnp.zeros_like(score_tiles))
    return lax.psum_scatter(score_tiles, "layer", scatter_dimension=0, tiled=True)


def halves(x):
    hi = x.astype(bf16)
    return hi, (x - hi.astype(f32)).astype(bf16)


def nn(a, b):
    return lax.dot_general(a, b, (((1,), (0,)), ((), ())), preferred_element_type=f32)


def nt(a, b):
    return lax.dot_general(a, b, (((1,), (1,)), ((), ())), preferred_element_type=f32)


def one_hot(hits):
    return jnp.where(hits, 1.0, 0.0).astype(bf16)


def iota(shape, dim):
    return lax.broadcasted_iota(jnp.int32, shape, dim)


def stacked(x):
    hi, lo = halves(x)
    return jnp.concatenate([hi, lo, hi], axis=0)


def write_own_rows(q_ref, bi_ref, bo_ref, ev_ref, mask_ref, xs, gath, me, ready, send_rows):
    for j in range(32):
        xs[32 * j : 32 * j + 32, :] = q_ref[0, :, 128 * j : 128 * j + 128].astype(f32)
    r, c = iota((256, 256), 0), iota((256, 256), 1)
    same = (r // 128 == (c // 64) % 2) & ((r // 64) % 2 == c // 128)
    put_a = one_hot(iota((256, 64), 0) % 64 == iota((256, 64), 1))
    wa = [
        jnp.where(same, nt(nn(put_a, part).astype(bf16), put_a), 0.0).astype(bf16)
        for part in halves(bi_ref[0])
    ]
    row = iota((64, 64), 0)
    put_b = one_hot(2 * (row % 32) + row // 32 == iota((64, 64), 1))
    col = iota((192, 64), 0)
    order = 2 * (col % 32) + (col // 32) % 2 == iota((192, 64), 1)
    place = [one_hot(order & (col < 128)), one_hot(order & (col >= 128))]
    wb, wc = 0.0, 0.0
    for part, to in zip(halves(bo_ref[0]), place):
        wb = wb + nt(nt(put_b, part).astype(bf16), to)
        wc = wc + nt(nn(put_b, part).astype(bf16), to)
    wb, wc = wb.astype(bf16), wc.astype(bf16)
    inverse = 1.0 / (ev_ref[0] + damping)
    top = inverse.astype(bf16)
    scale = 0.0
    for part in (top,) + halves(inverse - top.astype(f32)):
        scale = scale + nt(nn(put_b, part).astype(bf16), put_a[:128])
    scale = jnp.concatenate([scale] * 16, axis=1)

    block = jnp.concatenate(
        [
            jnp.concatenate(
                [xs[pl.ds(q + 16 * g, 32, stride=32), :] for g in range(2)], axis=1
            )
            for q in range(16)
        ],
        axis=0,
    ).astype(bf16)
    turned = nn(block, wa[0]) + nn(block, wa[1])
    s = jnp.concatenate(
        [
            jnp.concatenate(
                [turned[32 * q : 32 * q + 32, 128 * p : 128 * p + 128] for p in range(2)], axis=0
            )
            for q in range(16)
        ],
        axis=1,
    )
    rotated = nn(wb, stacked(s))
    v = nn(wc, stacked(rotated * scale))
    y = jnp.concatenate(
        [
            jnp.concatenate(
                [v[32 * p : 32 * p + 32, 128 * q : 128 * q + 128] for p in range(2)], axis=1
            )
            for q in range(16)
        ],
        axis=0,
    )
    y_hi, y_lo = halves(y)
    done = nt(y_hi, wa[0]) + (nt(y_lo, wa[0]) + nt(y_hi, wa[1]))
    for q in range(16):
        for g in range(2):
            xs[pl.ds(q + 16 * g, 32, stride=32), :] = done[
                32 * q : 32 * q + 32, 128 * g : 128 * g + 128
            ]
    picked = iota((32, 256), 1) == me * 32 + iota((32, 256), 0)
    weights = jnp.sum(jnp.where(picked, mask_ref[...].astype(f32), 0.0), axis=1, keepdims=True)
    rows = pl.ds(pl.multiple_of(me * 32, 32), 32)
    ready()

    def chunk(k, carry):
        for j in range(8):
            tile = xs[pl.ds(pl.multiple_of(256 * k + 32 * j, 32), 32), :]
            gath[k, rows, 128 * j : 128 * j + 128] = (tile * weights).astype(bf16)
        send_rows(k)
        return carry

    lax.fori_loop(0, N_CHUNK, chunk, 0)


def kernel(
    nz, q_ref, stored_ref, bi_ref, bo_ref, ev_ref, mask_ref, out_ref,
    xs, st, gath, acc, sbuf, rbuf,
    st_sem, recv_sem, up_sem, down_sem, y_sem, rs_send, rs_recv,
):
    layers = sbuf.shape[0]
    width = st.shape[2]
    parts = sbuf.shape[1]
    me = lax.axis_index("doc")
    mine = lax.axis_index("layer")
    z, y = me // 2, me % 2
    partner = me + 1 - 2 * y

    def load(k):
        return pltpu.make_async_copy(
            stored_ref.at[0, :, pl.ds(k * width, width)], st.at[k], st_sem.at[k]
        )

    for k in range(N_CHUNK):
        load(k).start()

    barrier = pltpu.get_barrier_semaphore()
    pl.semaphore_signal(barrier, inc=1, device_id={"doc": partner}, device_id_type=MESH)
    for step in range(1, layers):
        pl.semaphore_signal(
            barrier, inc=1, device_id={"layer": lax.rem(mine + step, layers)}, device_id_type=MESH
        )

    @pl.when(z < nz - 1)
    def _():
        pl.semaphore_signal(barrier, inc=1, device_id={"doc": me + 2}, device_id_type=MESH)

    @pl.when(z > 0)
    def _():
        pl.semaphore_signal(barrier, inc=1, device_id={"doc": me - 2}, device_id_type=MESH)

    def plane_at(s):
        far = (z >= 2).astype(jnp.int32)
        near = z + far * (3 - 2 * z)
        inner = (near == 1).astype(jnp.int32)
        swap = inner * jnp.where(s < 2, 1, 0)
        p = s + swap * (1 - 2 * s)
        return p + far * (3 - 2 * p)

    def send(p, side, k, sems, target):
        blk = 2 * p + side
        part = gath.at[k, pl.ds(pl.multiple_of(blk * 32, 32), 32)]
        return pltpu.make_async_remote_copy(
            src_ref=part, dst_ref=part, send_sem=sems.at[blk, k], recv_sem=recv_sem.at[blk, k],
            device_id={"doc": target}, device_id_type=MESH,
        )

    def up(p, side, k):
        return send(p, side, k, up_sem, me + 2)

    def down(p, side, k):
        return send(p, side, k, down_sem, me - 2)

    def across(p, k):
        return send(p, y, k, y_sem, partner)

    def landed(p, side, k):
        return send(p, side, k, y_sem, partner)

    def both_columns(p, k):
        return ((p == 0) | (p == nz - 1)) & (k % 2 == 1)

    def goes_up(p):
        return (p <= z) & (z < nz - 1)

    def goes_down(p):
        return (p >= z) & (z > 0)

    def goes_across(p, k):
        return (p == z) | jnp.logical_not(both_columns(p, k))

    def relayed(p, k):
        return both_columns(p, k) & (p != z) & (p + z != nz - 1)

    def forward(t):
        p, k = plane_at(t // N_CHUNK), t % N_CHUNK

        landed(p, y, k).wait_recv()

        @pl.when(goes_up(p))
        def _():
            up(p, y, k).start()

        @pl.when(goes_down(p))
        def _():
            down(p, y, k).start()

        @pl.when(jnp.logical_not(both_columns(p, k)))
        def _():
            across(p, k).start()

    def send_rows(k):
        @pl.when(z < nz - 1)
        def _():
            up(z, y, k).start()

        @pl.when(z > 0)
        def _():
            down(z, y, k).start()

        across(z, k).start()

    def ready():
        ends = jnp.where(z == 0, 1, 0) + jnp.where(z == nz - 1, 1, 0)
        pl.semaphore_wait(barrier, layers + 2 - ends)

    def pass_on(p, k):
        @pl.when(goes_up(p))
        def _():
            up(p, 1 - y, k).start()

        @pl.when(goes_down(p))
        def _():
            down(p, 1 - y, k).start()

    def relay(t):
        p, k = plane_at(t // N_CHUNK), t % N_CHUNK

        @pl.when(relayed(p, k))
        def _():
            landed(p, 1 - y, k).wait_recv()
            pass_on(p, k)

    def hand_over(p, s, n):
        return pltpu.make_async_remote_copy(
            src_ref=sbuf.at[s, n], dst_ref=rbuf.at[mine, n], send_sem=rs_send.at[s, n],
            recv_sem=rs_recv.at[mine, n], device_id={"layer": p}, device_id_type=MESH,
        )

    def compute(t):
        s, k = t // N_CHUNK, t % N_CHUNK
        p = plane_at(s)

        @pl.when(jnp.logical_not(relayed(p, k)))
        def _():
            landed(p, 1 - y, k).wait_recv()

        @pl.when((s == 0) & both_columns(p, k))
        def _():
            pass_on(p, k)

        @pl.when(s == 0)
        def _():
            load(k).wait()

        rows = pl.ds(pl.multiple_of(p * 64, 64), 64)

        @pl.when(k == 0)
        def _():
            acc[...] = jnp.zeros_like(acc)

        @pl.when(k < N_CHUNK - 1)
        def _():
            acc[...] += nt(gath[k, rows, :], st[k])

        @pl.when(k == N_CHUNK - 1)
        def _():
            def column(n, carry):
                cols = pl.ds(pl.multiple_of(n * 256, 256), 256)
                total = acc[:, cols] + nt(gath[k, rows, :], st[k, cols, :])

                @pl.when(p == mine)
                def _():
                    out_ref[:, cols] = total

                @pl.when(p != mine)
                def _():
                    sbuf[s, n] = total.astype(bf16)
                    hand_over(p, s, n).start()

                return carry

            lax.fori_loop(0, parts, column, 0)

    steps = nz * N_CHUNK

    def first(t, carry):
        forward(t)
        return carry

    def body(t, carry):
        @pl.when(t + lead < steps)
        def _():
            forward(t + lead)

        @pl.when(t + 2 < steps)
        def _():
            relay(t + 2)

        compute(t)
        return carry

    write_own_rows(q_ref, bi_ref, bo_ref, ev_ref, mask_ref, xs, gath, me, ready, send_rows)
    lead = N_CHUNK * jnp.where((z == 0) | (z == nz - 1), 1, 2)
    lax.fori_loop(N_CHUNK, lead, first, 0)
    lax.fori_loop(0, steps, body, 0)

    def collect(n, carry):
        cols = pl.ds(pl.multiple_of(n * 256, 256), 256)
        total = out_ref[:, cols]
        for step in range(1, layers):
            other = lax.rem(mine + step, layers)
            pltpu.make_async_remote_copy(
                src_ref=sbuf.at[0, n], dst_ref=rbuf.at[other, n], send_sem=rs_send.at[0, n],
                recv_sem=rs_recv.at[other, n], device_id={"layer": other}, device_id_type=MESH,
            ).wait_recv()
            total = total + rbuf[other, n].astype(f32)
        out_ref[:, cols] = total
        return carry

    lax.fori_loop(0, parts, collect, 0)

    def drain(t, carry):
        p, k = t // N_CHUNK, t % N_CHUNK

        @pl.when(goes_up(p))
        def _():
            up(p, y, k).wait_send()

        @pl.when(goes_down(p))
        def _():
            down(p, y, k).wait_send()

        @pl.when(both_columns(p, k) & goes_up(p))
        def _():
            up(p, 1 - y, k).wait_send()

        @pl.when(both_columns(p, k) & goes_down(p))
        def _():
            down(p, 1 - y, k).wait_send()

        @pl.when(goes_across(p, k))
        def _():
            across(p, k).wait_send()

        return carry

    lax.fori_loop(0, steps, drain, 0)

    def drain_scores(t, carry):
        s, n = t // parts, t % parts
        p = plane_at(s)

        @pl.when(p != mine)
        def _():
            hand_over(p, s, n).wait_send()

        return carry

    lax.fori_loop(0, nz * parts, drain_scores, 0)


def in_one_kernel(nz, query_grads, stored_grads, basis_in, basis_out, eigen_values, layer_mask, doc_counts):
    layers = nz
    _, docs, depth = stored_grads.shape
    queries = layer_mask.shape[0]
    rows = queries // layers
    width = depth // N_CHUNK
    vmem = pl.BlockSpec(memory_space=pltpu.VMEM)
    summed = pl.pallas_call(
        functools.partial(kernel, nz),
        out_shape=jax.ShapeDtypeStruct((rows, docs), f32),
        in_specs=[vmem, pl.BlockSpec(memory_space=pltpu.HBM), vmem, vmem, vmem, vmem],
        out_specs=vmem,
        scratch_shapes=[
            pltpu.VMEM((depth * query_grads.shape[1] // 128, 128), f32),
            pltpu.VMEM((N_CHUNK, docs, width), bf16),
            pltpu.VMEM((N_CHUNK, queries, width), bf16),
            pltpu.VMEM((rows, docs), f32),
            pltpu.VMEM((nz, docs // 256, rows, 256), bf16),
            pltpu.VMEM((layers, docs // 256, rows, 256), bf16),
            pltpu.SemaphoreType.DMA((N_CHUNK,)),
            pltpu.SemaphoreType.DMA((2 * nz, N_CHUNK)),
            pltpu.SemaphoreType.DMA((2 * nz, N_CHUNK)),
            pltpu.SemaphoreType.DMA((2 * nz, N_CHUNK)),
            pltpu.SemaphoreType.DMA((2 * nz, N_CHUNK)),
            pltpu.SemaphoreType.DMA((nz, docs // 256)),
            pltpu.SemaphoreType.DMA((layers, docs // 256)),
        ],
        compiler_params=pltpu.CompilerParams(
            collective_id=0, has_side_effects=True, vmem_limit_bytes=58 * 1024 * 1024
        ),
        cost_estimate=pl.CostEstimate(
            flops=2 * queries * docs * depth, bytes_accessed=2 * docs * depth, transcendentals=0
        ),
    )(query_grads, stored_grads, basis_in, basis_out, eigen_values, layer_mask.reshape(1, queries))
    live_slots = jnp.arange(docs, dtype=jnp.int32) < doc_counts[0]
    return jnp.where(live_slots[None, :], summed, jnp.zeros_like(summed))


def on_device(query_grads, stored_grads, *rest):
    n_doc, layers = lax.axis_size("doc"), lax.axis_size("layer")
    shape = query_grads.shape
    if n_doc == 8 and layers == 4 and shape == (1, 32, 4096):
        return in_one_kernel(n_doc // 2, query_grads, stored_grads, *rest)
    return by_collectives(query_grads, stored_grads, *rest)


def solution(mesh):
    in_specs = (
        P("layer", "doc", None),
        P("layer", "doc", None),
        P("layer", None, None),
        P("layer", None, None),
        P("layer", None, None),
        P(None, "layer"),
        P("doc"),
    )
    out_specs = P("layer", "doc")
    return jax.shard_map(
        on_device, mesh=mesh, in_specs=in_specs, out_specs=out_specs, check_vma=False
    )
```

```python
import functools
import jax
import jax.numpy as jnp
from jax import lax
from jax.experimental import pallas as pl
from jax.experimental.pallas import tpu as pltpu
from jax.sharding import PartitionSpec as P

damping = 0.1
N_CHUNK = 4
MESH = pl.DeviceIdType.MESH
f32 = jnp.float32
bf16 = jnp.bfloat16


def precondition(gradients, basis_in, basis_out, eigen_values):
    row_count = gradients.shape[0]
    grid_blocks = gradients.astype(jnp.float32).reshape(
        row_count, basis_out.shape[0], basis_in.shape[0]
    )
    rotated = jnp.einsum(
        "xi,qxy,yj->qij", basis_out, grid_blocks, basis_in, precision=lax.Precision.HIGHEST
    )
    scaled = rotated / (eigen_values + damping)
    restored = jnp.einsum(
        "bi,qij,aj->qba", basis_out, scaled, basis_in, precision=lax.Precision.HIGHEST
    )
    return restored.reshape(row_count, -1).astype(jnp.bfloat16)


def by_collectives(query_grads, stored_grads, basis_in, basis_out, eigen_values, layer_mask, doc_counts):
    stored = stored_grads[0]
    row_weights = layer_mask[:, 0].astype(jnp.bfloat16)
    own_rows = precondition(query_grads[0], basis_in[0], basis_out[0], eigen_values[0])
    masked = lax.all_gather(own_rows, "doc", axis=0, tiled=True) * row_weights[:, None]
    score_tiles = lax.dot_general(
        masked, stored, (((1,), (1,)), ((), ())), preferred_element_type=jnp.float32
    )
    live_slots = jnp.arange(stored.shape[0], dtype=jnp.int32) < doc_counts[0]
    score_tiles = jnp.where(live_slots[None, :], score_tiles, jnp.zeros_like(score_tiles))
    return lax.psum_scatter(score_tiles, "layer", scatter_dimension=0, tiled=True)


def halves(x):
    hi = x.astype(bf16)
    return hi, (x - hi.astype(f32)).astype(bf16)


def nn(a, b):
    return lax.dot_general(a, b, (((1,), (0,)), ((), ())), preferred_element_type=f32)


def nt(a, b):
    return lax.dot_general(a, b, (((1,), (1,)), ((), ())), preferred_element_type=f32)


def one_hot(hits):
    return jnp.where(hits, 1.0, 0.0).astype(bf16)


def iota(shape, dim):
    return lax.broadcasted_iota(jnp.int32, shape, dim)


def stacked(x):
    hi, lo = halves(x)
    return jnp.concatenate([hi, lo, hi], axis=0)


def write_own_rows(q_ref, bi_ref, bo_ref, ev_ref, mask_ref, xs, gath, me, ready, send_rows):
    for j in range(32):
        xs[32 * j : 32 * j + 32, :] = q_ref[0, :, 128 * j : 128 * j + 128].astype(f32)
    r, c = iota((256, 256), 0), iota((256, 256), 1)
    same = (r // 128 == (c // 64) % 2) & ((r // 64) % 2 == c // 128)
    put_a = one_hot(iota((256, 64), 0) % 64 == iota((256, 64), 1))
    wa = [
        jnp.where(same, nt(nn(put_a, part).astype(bf16), put_a), 0.0).astype(bf16)
        for part in halves(bi_ref[0])
    ]
    row = iota((64, 64), 0)
    put_b = one_hot(2 * (row % 32) + row // 32 == iota((64, 64), 1))
    col = iota((192, 64), 0)
    order = 2 * (col % 32) + (col // 32) % 2 == iota((192, 64), 1)
    place = [one_hot(order & (col < 128)), one_hot(order & (col >= 128))]
    wb, wc = 0.0, 0.0
    for part, to in zip(halves(bo_ref[0]), place):
        wb = wb + nt(nt(put_b, part).astype(bf16), to)
        wc = wc + nt(nn(put_b, part).astype(bf16), to)
    wb, wc = wb.astype(bf16), wc.astype(bf16)
    inverse = 1.0 / (ev_ref[0] + damping)
    top = inverse.astype(bf16)
    scale = 0.0
    for part in (top,) + halves(inverse - top.astype(f32)):
        scale = scale + nt(nn(put_b, part).astype(bf16), put_a[:128])
    scale = jnp.concatenate([scale] * 16, axis=1)

    block = jnp.concatenate(
        [
            jnp.concatenate(
                [xs[pl.ds(q + 16 * g, 32, stride=32), :] for g in range(2)], axis=1
            )
            for q in range(16)
        ],
        axis=0,
    ).astype(bf16)
    turned = nn(block, wa[0]) + nn(block, wa[1])
    s = jnp.concatenate(
        [
            jnp.concatenate(
                [turned[32 * q : 32 * q + 32, 128 * p : 128 * p + 128] for p in range(2)], axis=0
            )
            for q in range(16)
        ],
        axis=1,
    )
    rotated = nn(wb, stacked(s))
    v = nn(wc, stacked(rotated * scale))
    y = jnp.concatenate(
        [
            jnp.concatenate(
                [v[32 * p : 32 * p + 32, 128 * q : 128 * q + 128] for p in range(2)], axis=1
            )
            for q in range(16)
        ],
        axis=0,
    )
    y_hi, y_lo = halves(y)
    done = nt(y_hi, wa[0]) + (nt(y_lo, wa[0]) + nt(y_hi, wa[1]))
    for q in range(16):
        for g in range(2):
            xs[pl.ds(q + 16 * g, 32, stride=32), :] = done[
                32 * q : 32 * q + 32, 128 * g : 128 * g + 128
            ]
    picked = iota((32, 256), 1) == me * 32 + iota((32, 256), 0)
    weights = jnp.sum(jnp.where(picked, mask_ref[...].astype(f32), 0.0), axis=1, keepdims=True)
    rows = pl.ds(pl.multiple_of(me * 32, 32), 32)
    ready()

    def chunk(k, carry):
        for j in range(8):
            tile = xs[pl.ds(pl.multiple_of(256 * k + 32 * j, 32), 32), :]
            gath[k, rows, 128 * j : 128 * j + 128] = (tile * weights).astype(bf16)
        send_rows(k)
        return carry

    lax.fori_loop(0, N_CHUNK, chunk, 0)


def kernel(
    nz, q_ref, stored_ref, bi_ref, bo_ref, ev_ref, mask_ref, out_ref,
    xs, st, gath, acc, sbuf, rbuf,
    st_sem, recv_sem, up_sem, down_sem, y_sem, rs_send, rs_recv,
):
    layers = sbuf.shape[0]
    width = st.shape[2]
    parts = sbuf.shape[1]
    me = lax.axis_index("doc")
    mine = lax.axis_index("layer")
    z, y = me // 2, me % 2
    partner = me + 1 - 2 * y

    def load(k):
        return pltpu.make_async_copy(
            stored_ref.at[0, :, pl.ds(k * width, width)], st.at[k], st_sem.at[k]
        )

    for k in range(N_CHUNK):
        load(k).start()

    barrier = pltpu.get_barrier_semaphore()
    pl.semaphore_signal(barrier, inc=1, device_id={"doc": partner}, device_id_type=MESH)
    for step in range(1, layers):
        pl.semaphore_signal(
            barrier, inc=1, device_id={"layer": lax.rem(mine + step, layers)}, device_id_type=MESH
        )

    @pl.when(z < nz - 1)
    def _():
        pl.semaphore_signal(barrier, inc=1, device_id={"doc": me + 2}, device_id_type=MESH)

    @pl.when(z > 0)
    def _():
        pl.semaphore_signal(barrier, inc=1, device_id={"doc": me - 2}, device_id_type=MESH)

    def plane_at(s):
        far = (z >= 2).astype(jnp.int32)
        near = z + far * (3 - 2 * z)
        inner = (near == 1).astype(jnp.int32)
        swap = inner * jnp.where(s < 2, 1, 0)
        p = s + swap * (1 - 2 * s)
        return p + far * (3 - 2 * p)

    def send(p, side, k, sems, target):
        blk = 2 * p + side
        part = gath.at[k, pl.ds(pl.multiple_of(blk * 32, 32), 32)]
        return pltpu.make_async_remote_copy(
            src_ref=part, dst_ref=part, send_sem=sems.at[blk, k], recv_sem=recv_sem.at[blk, k],
            device_id={"doc": target}, device_id_type=MESH,
        )

    def up(p, side, k):
        return send(p, side, k, up_sem, me + 2)

    def down(p, side, k):
        return send(p, side, k, down_sem, me - 2)

    def across(p, k):
        return send(p, y, k, y_sem, partner)

    def landed(p, side, k):
        return send(p, side, k, y_sem, partner)

    def both_columns(p, k):
        return ((p == 0) | (p == nz - 1)) & (k % 2 == 1)

    def goes_up(p):
        return (p <= z) & (z < nz - 1)

    def goes_down(p):
        return (p >= z) & (z > 0)

    def goes_across(p, k):
        return (p == z) | jnp.logical_not(both_columns(p, k))

    def relayed(p, k):
        return both_columns(p, k) & (p != z) & (p + z != nz - 1)

    def forward(t):
        p, k = plane_at(t // N_CHUNK), t % N_CHUNK

        landed(p, y, k).wait_recv()

        @pl.when(goes_up(p))
        def _():
            up(p, y, k).start()

        @pl.when(goes_down(p))
        def _():
            down(p, y, k).start()

        @pl.when(jnp.logical_not(both_columns(p, k)))
        def _():
            across(p, k).start()

    def send_rows(k):
        @pl.when(z < nz - 1)
        def _():
            up(z, y, k).start()

        @pl.when(z > 0)
        def _():
            down(z, y, k).start()

        across(z, k).start()

    def ready():
        ends = jnp.where(z == 0, 1, 0) + jnp.where(z == nz - 1, 1, 0)
        pl.semaphore_wait(barrier, layers + 2 - ends)

    def pass_on(p, k):
        @pl.when(goes_up(p))
        def _():
            up(p, 1 - y, k).start()

        @pl.when(goes_down(p))
        def _():
            down(p, 1 - y, k).start()

    def relay(t):
        p, k = plane_at(t // N_CHUNK), t % N_CHUNK

        @pl.when(relayed(p, k))
        def _():
            landed(p, 1 - y, k).wait_recv()
            pass_on(p, k)

    def hand_over(p, s, n):
        return pltpu.make_async_remote_copy(
            src_ref=sbuf.at[s, n], dst_ref=rbuf.at[mine, n], send_sem=rs_send.at[s, n],
            recv_sem=rs_recv.at[mine, n], device_id={"layer": p}, device_id_type=MESH,
        )

    def compute(t):
        s, k = t // N_CHUNK, t % N_CHUNK
        p = plane_at(s)

        @pl.when(jnp.logical_not(relayed(p, k)))
        def _():
            landed(p, 1 - y, k).wait_recv()

        @pl.when((s == 0) & both_columns(p, k))
        def _():
            pass_on(p, k)

        @pl.when(s == 0)
        def _():
            load(k).wait()

        rows = pl.ds(pl.multiple_of(p * 64, 64), 64)

        @pl.when(k == 0)
        def _():
            acc[...] = jnp.zeros_like(acc)

        @pl.when(k < N_CHUNK - 1)
        def _():
            acc[...] += nt(st[k], gath[k, rows, :])

        @pl.when(k == N_CHUNK - 1)
        def _():
            def column(n, carry):
                cols = pl.ds(pl.multiple_of(n * 256, 256), 256)
                total = (acc[cols, :] + nt(st[k, cols, :], gath[k, rows, :])).T

                @pl.when(p == mine)
                def _():
                    out_ref[:, cols] = total

                @pl.when(p != mine)
                def _():
                    sbuf[s, n] = total.astype(bf16)
                    hand_over(p, s, n).start()

                return carry

            lax.fori_loop(0, parts, column, 0)

    steps = nz * N_CHUNK

    def first(t, carry):
        forward(t)
        return carry

    def body(t, carry):
        @pl.when(t + lead < steps)
        def _():
            forward(t + lead)

        @pl.when(t + 2 < steps)
        def _():
            relay(t + 2)

        compute(t)
        return carry

    write_own_rows(q_ref, bi_ref, bo_ref, ev_ref, mask_ref, xs, gath, me, ready, send_rows)
    lead = N_CHUNK * jnp.where((z == 0) | (z == nz - 1), 1, 2)
    lax.fori_loop(N_CHUNK, lead, first, 0)
    lax.fori_loop(0, steps, body, 0)

    def collect(n, carry):
        cols = pl.ds(pl.multiple_of(n * 256, 256), 256)
        total = out_ref[:, cols]
        for step in range(1, layers):
            other = lax.rem(mine + step, layers)
            pltpu.make_async_remote_copy(
                src_ref=sbuf.at[0, n], dst_ref=rbuf.at[other, n], send_sem=rs_send.at[0, n],
                recv_sem=rs_recv.at[other, n], device_id={"layer": other}, device_id_type=MESH,
            ).wait_recv()
            total = total + rbuf[other, n].astype(f32)
        out_ref[:, cols] = total
        return carry

    lax.fori_loop(0, parts, collect, 0)

    def drain(t, carry):
        p, k = t // N_CHUNK, t % N_CHUNK

        @pl.when(goes_up(p))
        def _():
            up(p, y, k).wait_send()

        @pl.when(goes_down(p))
        def _():
            down(p, y, k).wait_send()

        @pl.when(both_columns(p, k) & goes_up(p))
        def _():
            up(p, 1 - y, k).wait_send()

        @pl.when(both_columns(p, k) & goes_down(p))
        def _():
            down(p, 1 - y, k).wait_send()

        @pl.when(goes_across(p, k))
        def _():
            across(p, k).wait_send()

        return carry

    lax.fori_loop(0, steps, drain, 0)

    def drain_scores(t, carry):
        s, n = t // parts, t % parts
        p = plane_at(s)

        @pl.when(p != mine)
        def _():
            hand_over(p, s, n).wait_send()

        return carry

    lax.fori_loop(0, nz * parts, drain_scores, 0)


def in_one_kernel(nz, query_grads, stored_grads, basis_in, basis_out, eigen_values, layer_mask, doc_counts):
    layers = nz
    _, docs, depth = stored_grads.shape
    queries = layer_mask.shape[0]
    rows = queries // layers
    width = depth // N_CHUNK
    vmem = pl.BlockSpec(memory_space=pltpu.VMEM)
    summed = pl.pallas_call(
        functools.partial(kernel, nz),
        out_shape=jax.ShapeDtypeStruct((rows, docs), f32),
        in_specs=[vmem, pl.BlockSpec(memory_space=pltpu.HBM), vmem, vmem, vmem, vmem],
        out_specs=vmem,
        scratch_shapes=[
            pltpu.VMEM((depth * query_grads.shape[1] // 128, 128), f32),
            pltpu.VMEM((N_CHUNK, docs, width), bf16),
            pltpu.VMEM((N_CHUNK, queries, width), bf16),
            pltpu.VMEM((docs, rows), f32),
            pltpu.VMEM((nz, docs // 256, rows, 256), bf16),
            pltpu.VMEM((layers, docs // 256, rows, 256), bf16),
            pltpu.SemaphoreType.DMA((N_CHUNK,)),
            pltpu.SemaphoreType.DMA((2 * nz, N_CHUNK)),
            pltpu.SemaphoreType.DMA((2 * nz, N_CHUNK)),
            pltpu.SemaphoreType.DMA((2 * nz, N_CHUNK)),
            pltpu.SemaphoreType.DMA((2 * nz, N_CHUNK)),
            pltpu.SemaphoreType.DMA((nz, docs // 256)),
            pltpu.SemaphoreType.DMA((layers, docs // 256)),
        ],
        compiler_params=pltpu.CompilerParams(
            collective_id=0, has_side_effects=True, vmem_limit_bytes=58 * 1024 * 1024
        ),
        cost_estimate=pl.CostEstimate(
            flops=2 * queries * docs * depth, bytes_accessed=2 * docs * depth, transcendentals=0
        ),
    )(query_grads, stored_grads, basis_in, basis_out, eigen_values, layer_mask.reshape(1, queries))
    live_slots = jnp.arange(docs, dtype=jnp.int32) < doc_counts[0]
    return jnp.where(live_slots[None, :], summed, jnp.zeros_like(summed))


def on_device(query_grads, stored_grads, *rest):
    n_doc, layers = lax.axis_size("doc"), lax.axis_size("layer")
    shape = query_grads.shape
    if n_doc == 8 and layers == 4 and shape == (1, 32, 4096):
        return in_one_kernel(n_doc // 2, query_grads, stored_grads, *rest)
    return by_collectives(query_grads, stored_grads, *rest)


def solution(mesh):
    in_specs = (
        P("layer", "doc", None),
        P("layer", "doc", None),
        P("layer", None, None),
        P("layer", None, None),
        P("layer", None, None),
        P(None, "layer"),
        P("doc"),
    )
    out_specs = P("layer", "doc")
    return jax.shard_map(
        on_device, mesh=mesh, in_specs=in_specs, out_specs=out_specs, check_vma=False
    )
```

```python
import functools
import jax
import jax.numpy as jnp
from jax import lax
from jax.experimental import pallas as pl
from jax.experimental.pallas import tpu as pltpu
from jax.sharding import PartitionSpec as P

damping = 0.1
N_CHUNK = 4
MESH = pl.DeviceIdType.MESH
f32 = jnp.float32
bf16 = jnp.bfloat16


def precondition(gradients, basis_in, basis_out, eigen_values):
    row_count = gradients.shape[0]
    grid_blocks = gradients.astype(jnp.float32).reshape(
        row_count, basis_out.shape[0], basis_in.shape[0]
    )
    rotated = jnp.einsum(
        "xi,qxy,yj->qij", basis_out, grid_blocks, basis_in, precision=lax.Precision.HIGHEST
    )
    scaled = rotated / (eigen_values + damping)
    restored = jnp.einsum(
        "bi,qij,aj->qba", basis_out, scaled, basis_in, precision=lax.Precision.HIGHEST
    )
    return restored.reshape(row_count, -1).astype(jnp.bfloat16)


def by_collectives(query_grads, stored_grads, basis_in, basis_out, eigen_values, layer_mask, doc_counts):
    stored = stored_grads[0]
    row_weights = layer_mask[:, 0].astype(jnp.bfloat16)
    own_rows = precondition(query_grads[0], basis_in[0], basis_out[0], eigen_values[0])
    masked = lax.all_gather(own_rows, "doc", axis=0, tiled=True) * row_weights[:, None]
    score_tiles = lax.dot_general(
        masked, stored, (((1,), (1,)), ((), ())), preferred_element_type=jnp.float32
    )
    live_slots = jnp.arange(stored.shape[0], dtype=jnp.int32) < doc_counts[0]
    score_tiles = jnp.where(live_slots[None, :], score_tiles, jnp.zeros_like(score_tiles))
    return lax.psum_scatter(score_tiles, "layer", scatter_dimension=0, tiled=True)


def halves(x):
    hi = x.astype(bf16)
    return hi, (x - hi.astype(f32)).astype(bf16)


def nn(a, b):
    return lax.dot_general(a, b, (((1,), (0,)), ((), ())), preferred_element_type=f32)


def nt(a, b):
    return lax.dot_general(a, b, (((1,), (1,)), ((), ())), preferred_element_type=f32)


def one_hot(hits):
    return jnp.where(hits, 1.0, 0.0).astype(bf16)


def iota(shape, dim):
    return lax.broadcasted_iota(jnp.int32, shape, dim)


def stacked(x):
    hi, lo = halves(x)
    return jnp.concatenate([hi, lo, hi], axis=0)


def write_own_rows(q_ref, bi_ref, bo_ref, ev_ref, mask_ref, xs, gath, me, ready, send_rows):
    for j in range(32):
        xs[32 * j : 32 * j + 32, :] = q_ref[0, :, 128 * j : 128 * j + 128].astype(f32)
    r, c = iota((256, 256), 0), iota((256, 256), 1)
    same = (r // 128 == (c // 64) % 2) & ((r // 64) % 2 == c // 128)
    put_a = one_hot(iota((256, 64), 0) % 64 == iota((256, 64), 1))
    wa = [
        jnp.where(same, nt(nn(put_a, part).astype(bf16), put_a), 0.0).astype(bf16)
        for part in halves(bi_ref[0])
    ]
    row = iota((64, 64), 0)
    put_b = one_hot(2 * (row % 32) + row // 32 == iota((64, 64), 1))
    col = iota((192, 64), 0)
    order = 2 * (col % 32) + (col // 32) % 2 == iota((192, 64), 1)
    place = [one_hot(order & (col < 128)), one_hot(order & (col >= 128))]
    wb, wc = 0.0, 0.0
    for part, to in zip(halves(bo_ref[0]), place):
        wb = wb + nt(nt(put_b, part).astype(bf16), to)
        wc = wc + nt(nn(put_b, part).astype(bf16), to)
    wb, wc = wb.astype(bf16), wc.astype(bf16)
    inverse = 1.0 / (ev_ref[0] + damping)
    top = inverse.astype(bf16)
    scale = 0.0
    for part in (top,) + halves(inverse - top.astype(f32)):
        scale = scale + nt(nn(put_b, part).astype(bf16), put_a[:128])
    scale = jnp.concatenate([scale] * 16, axis=1)

    block = jnp.concatenate(
        [
            jnp.concatenate(
                [xs[pl.ds(q + 16 * g, 32, stride=32), :] for g in range(2)], axis=1
            )
            for q in range(16)
        ],
        axis=0,
    ).astype(bf16)
    turned = nn(block, wa[0]) + nn(block, wa[1])
    s = jnp.concatenate(
        [
            jnp.concatenate(
                [turned[32 * q : 32 * q + 32, 128 * p : 128 * p + 128] for p in range(2)], axis=0
            )
            for q in range(16)
        ],
        axis=1,
    )
    rotated = nn(wb, stacked(s))
    v = nn(wc, stacked(rotated * scale))
    y = jnp.concatenate(
        [
            jnp.concatenate(
                [v[32 * p : 32 * p + 32, 128 * q : 128 * q + 128] for p in range(2)], axis=1
            )
            for q in range(16)
        ],
        axis=0,
    )
    y_hi, y_lo = halves(y)
    done = nt(y_hi, wa[0]) + (nt(y_lo, wa[0]) + nt(y_hi, wa[1]))
    for q in range(16):
        for g in range(2):
            xs[pl.ds(q + 16 * g, 32, stride=32), :] = done[
                32 * q : 32 * q + 32, 128 * g : 128 * g + 128
            ]
    picked = iota((32, 256), 1) == me * 32 + iota((32, 256), 0)
    weights = jnp.sum(jnp.where(picked, mask_ref[...].astype(f32), 0.0), axis=1, keepdims=True)
    rows = pl.ds(pl.multiple_of(me * 32, 32), 32)
    ready()

    def chunk(k, carry):
        for j in range(8):
            tile = xs[pl.ds(pl.multiple_of(256 * k + 32 * j, 32), 32), :]
            gath[k, rows, 128 * j : 128 * j + 128] = (tile * weights).astype(bf16)
        send_rows(k)
        return carry

    lax.fori_loop(0, N_CHUNK, chunk, 0)


def kernel(
    nz, q_ref, stored_ref, bi_ref, bo_ref, ev_ref, mask_ref, out_ref,
    xs, st, gath, acc, own, sbuf, rbuf,
    st_sem, recv_sem, up_sem, down_sem, y_sem, rs_send, rs_recv, out_sem,
):
    layers = sbuf.shape[0]
    width = st.shape[2]
    parts = sbuf.shape[1]
    me = lax.axis_index("doc")
    mine = lax.axis_index("layer")
    z, y = me // 2, me % 2
    partner = me + 1 - 2 * y

    def load(k):
        return pltpu.make_async_copy(
            stored_ref.at[0, :, pl.ds(k * width, width)], st.at[k], st_sem.at[k]
        )

    for k in range(N_CHUNK):
        load(k).start()

    barrier = pltpu.get_barrier_semaphore()
    pl.semaphore_signal(barrier, inc=1, device_id={"doc": partner}, device_id_type=MESH)
    for step in range(1, layers):
        pl.semaphore_signal(
            barrier, inc=1, device_id={"layer": lax.rem(mine + step, layers)}, device_id_type=MESH
        )

    @pl.when(z < nz - 1)
    def _():
        pl.semaphore_signal(barrier, inc=1, device_id={"doc": me + 2}, device_id_type=MESH)

    @pl.when(z > 0)
    def _():
        pl.semaphore_signal(barrier, inc=1, device_id={"doc": me - 2}, device_id_type=MESH)

    def plane_at(s):
        far = (z >= 2).astype(jnp.int32)
        near = z + far * (3 - 2 * z)
        inner = (near == 1).astype(jnp.int32)
        swap = inner * jnp.where(s < 2, 1, 0)
        p = s + swap * (1 - 2 * s)
        return p + far * (3 - 2 * p)

    def send(p, side, k, sems, target):
        blk = 2 * p + side
        part = gath.at[k, pl.ds(pl.multiple_of(blk * 32, 32), 32)]
        return pltpu.make_async_remote_copy(
            src_ref=part, dst_ref=part, send_sem=sems.at[blk, k], recv_sem=recv_sem.at[blk, k],
            device_id={"doc": target}, device_id_type=MESH,
        )

    def up(p, side, k):
        return send(p, side, k, up_sem, me + 2)

    def down(p, side, k):
        return send(p, side, k, down_sem, me - 2)

    def across(p, k):
        return send(p, y, k, y_sem, partner)

    def landed(p, side, k):
        return send(p, side, k, y_sem, partner)

    def both_columns(p, k):
        return ((p == 0) | (p == nz - 1)) & (k % 2 == 1)

    def goes_up(p):
        return (p <= z) & (z < nz - 1)

    def goes_down(p):
        return (p >= z) & (z > 0)

    def goes_across(p, k):
        return (p == z) | jnp.logical_not(both_columns(p, k))

    def relayed(p, k):
        return both_columns(p, k) & (p != z) & (p + z != nz - 1)

    def forward(t):
        p, k = plane_at(t // N_CHUNK), t % N_CHUNK

        landed(p, y, k).wait_recv()

        @pl.when(goes_up(p))
        def _():
            up(p, y, k).start()

        @pl.when(goes_down(p))
        def _():
            down(p, y, k).start()

        @pl.when(jnp.logical_not(both_columns(p, k)))
        def _():
            across(p, k).start()

    def send_rows(k):
        @pl.when(z < nz - 1)
        def _():
            up(z, y, k).start()

        @pl.when(z > 0)
        def _():
            down(z, y, k).start()

        across(z, k).start()

    def ready():
        ends = jnp.where(z == 0, 1, 0) + jnp.where(z == nz - 1, 1, 0)
        pl.semaphore_wait(barrier, layers + 2 - ends)

    def pass_on(p, k):
        @pl.when(goes_up(p))
        def _():
            up(p, 1 - y, k).start()

        @pl.when(goes_down(p))
        def _():
            down(p, 1 - y, k).start()

    def relay(t):
        p, k = plane_at(t // N_CHUNK), t % N_CHUNK

        @pl.when(relayed(p, k))
        def _():
            landed(p, 1 - y, k).wait_recv()
            pass_on(p, k)

    def hand_over(p, s, n, half=None):
        take = pl.ds(0, 64) if half is None else pl.ds(pl.multiple_of(half * 32, 32), 32)
        return pltpu.make_async_remote_copy(
            src_ref=sbuf.at[s, n, take], dst_ref=rbuf.at[mine, n, take],
            send_sem=rs_send.at[s, n], recv_sem=rs_recv.at[mine, n],
            device_id={"layer": p}, device_id_type=MESH,
        )

    def multiply(p, s, k, half=None):
        count = 64 if half is None else 32
        at = 0 if half is None else pl.multiple_of(half * 32, 32)
        rows = pl.ds(pl.multiple_of(p * 64 + at, 32), count)
        local = pl.ds(at, count)

        @pl.when(k == 0)
        def _():
            acc[local, :] = jnp.zeros((count, acc.shape[1]), f32)

        @pl.when(k < N_CHUNK - 1)
        def _():
            acc[local, :] += nt(gath[k, rows, :], st[k])

        @pl.when(k == N_CHUNK - 1)
        def _():
            def column(n, carry):
                cols = pl.ds(pl.multiple_of(n * 256, 256), 256)
                total = acc[local, cols] + nt(gath[k, rows, :], st[k, cols, :])

                @pl.when(p == mine)
                def _():
                    own[local, cols] = total

                @pl.when(p != mine)
                def _():
                    sbuf[s, n, local, :] = total.astype(bf16)
                    hand_over(p, s, n, half).start()

                return carry

            lax.fori_loop(0, parts, column, 0)

    def compute(t):
        s, k = t // N_CHUNK, t % N_CHUNK
        p = plane_at(s)

        @pl.when(jnp.logical_not(relayed(p, k)))
        def _():
            landed(p, 1 - y, k).wait_recv()

        @pl.when((s == 0) & both_columns(p, k))
        def _():
            pass_on(p, k)

        @pl.when(s == 0)
        def _():
            load(k).wait()

        multiply(p, s, k)

    steps = nz * N_CHUNK

    def first(t, carry):
        forward(t)
        return carry

    def body(t, carry):
        @pl.when(t + lead < steps)
        def _():
            forward(t + lead)

        @pl.when(t + 2 < steps)
        def _():
            relay(t + 2)

        compute(t)
        return carry

    write_own_rows(q_ref, bi_ref, bo_ref, ev_ref, mask_ref, xs, gath, me, ready, send_rows)
    lead = N_CHUNK * jnp.where((z == 0) | (z == nz - 1), 1, 2)
    lax.fori_loop(N_CHUNK, lead, first, 0)
    lax.fori_loop(0, steps - N_CHUNK, body, 0)
    relay(steps - 1)

    def last(t, carry):
        own_side, k = t // N_CHUNK == 0, t % N_CHUNK
        p = plane_at(nz - 1)
        side = jnp.where(own_side, y, 1 - y)

        @pl.when(jnp.logical_not(own_side | relayed(p, k)))
        def _():
            landed(p, 1 - y, k).wait_recv()

        multiply(p, nz - 1, k, side)
        return carry

    lax.fori_loop(0, 2 * N_CHUNK, last, 0)

    def drain(t, carry):
        p, k = t // N_CHUNK, t % N_CHUNK

        @pl.when(goes_up(p))
        def _():
            up(p, y, k).wait_send()

        @pl.when(goes_down(p))
        def _():
            down(p, y, k).wait_send()

        @pl.when(both_columns(p, k) & goes_up(p))
        def _():
            up(p, 1 - y, k).wait_send()

        @pl.when(both_columns(p, k) & goes_down(p))
        def _():
            down(p, 1 - y, k).wait_send()

        @pl.when(goes_across(p, k))
        def _():
            across(p, k).wait_send()

        return carry

    lax.fori_loop(0, steps, drain, 0)

    def drain_scores(t, carry):
        s, n = t // parts, t % parts
        p = plane_at(s)

        @pl.when(p != mine)
        def _():
            hand_over(p, s, n).wait_send()

        return carry

    lax.fori_loop(0, nz * parts, drain_scores, 0)

    def write(n):
        cols = pl.ds(n * 256 if isinstance(n, int) else pl.multiple_of(n * 256, 256), 256)
        return pltpu.make_async_copy(own.at[:, cols], out_ref.at[:, cols], out_sem.at[n])

    def collect(n, carry):
        cols = pl.ds(pl.multiple_of(n * 256, 256), 256)
        total = own[:, cols]
        for step in range(1, layers):
            other = lax.rem(mine + step, layers)
            pltpu.make_async_remote_copy(
                src_ref=sbuf.at[0, n], dst_ref=rbuf.at[other, n], send_sem=rs_send.at[0, n],
                recv_sem=rs_recv.at[other, n], device_id={"layer": other}, device_id_type=MESH,
            ).wait_recv()
            total = total + rbuf[other, n].astype(f32)
        own[:, cols] = total
        write(n).start()
        return carry

    lax.fori_loop(0, parts, collect, 0)
    for n in range(parts):
        write(n).wait()


def in_one_kernel(nz, query_grads, stored_grads, basis_in, basis_out, eigen_values, layer_mask, doc_counts):
    layers = nz
    _, docs, depth = stored_grads.shape
    queries = layer_mask.shape[0]
    rows = queries // layers
    width = depth // N_CHUNK
    vmem = pl.BlockSpec(memory_space=pltpu.VMEM)
    summed = pl.pallas_call(
        functools.partial(kernel, nz),
        out_shape=jax.ShapeDtypeStruct((rows, docs), f32),
        in_specs=[vmem, pl.BlockSpec(memory_space=pltpu.HBM), vmem, vmem, vmem, vmem],
        out_specs=pl.BlockSpec(memory_space=pl.ANY),
        scratch_shapes=[
            pltpu.VMEM((depth * query_grads.shape[1] // 128, 128), f32),
            pltpu.VMEM((N_CHUNK, docs, width), bf16),
            pltpu.VMEM((N_CHUNK, queries, width), bf16),
            pltpu.VMEM((rows, docs), f32),
            pltpu.VMEM((rows, docs), f32),
            pltpu.VMEM((nz, docs // 256, rows, 256), bf16),
            pltpu.VMEM((layers, docs // 256, rows, 256), bf16),
            pltpu.SemaphoreType.DMA((N_CHUNK,)),
            pltpu.SemaphoreType.DMA((2 * nz, N_CHUNK)),
            pltpu.SemaphoreType.DMA((2 * nz, N_CHUNK)),
            pltpu.SemaphoreType.DMA((2 * nz, N_CHUNK)),
            pltpu.SemaphoreType.DMA((2 * nz, N_CHUNK)),
            pltpu.SemaphoreType.DMA((nz, docs // 256)),
            pltpu.SemaphoreType.DMA((layers, docs // 256)),
            pltpu.SemaphoreType.DMA((docs // 256,)),
        ],
        compiler_params=pltpu.CompilerParams(
            collective_id=0, has_side_effects=True, vmem_limit_bytes=58 * 1024 * 1024
        ),
        cost_estimate=pl.CostEstimate(
            flops=2 * queries * docs * depth, bytes_accessed=2 * docs * depth, transcendentals=0
        ),
    )(query_grads, stored_grads, basis_in, basis_out, eigen_values, layer_mask.reshape(1, queries))
    live_slots = jnp.arange(docs, dtype=jnp.int32) < doc_counts[0]
    return jnp.where(live_slots[None, :], summed, jnp.zeros_like(summed))


def on_device(query_grads, stored_grads, *rest):
    n_doc, layers = lax.axis_size("doc"), lax.axis_size("layer")
    shape = query_grads.shape
    if n_doc == 8 and layers == 4 and shape == (1, 32, 4096):
        return in_one_kernel(n_doc // 2, query_grads, stored_grads, *rest)
    return by_collectives(query_grads, stored_grads, *rest)


def solution(mesh):
    in_specs = (
        P("layer", "doc", None),
        P("layer", "doc", None),
        P("layer", None, None),
        P("layer", None, None),
        P("layer", None, None),
        P(None, "layer"),
        P("doc"),
    )
    out_specs = P("layer", "doc")
    return jax.shard_map(
        on_device, mesh=mesh, in_specs=in_specs, out_specs=out_specs, check_vma=False
    )
```

```python
import functools
import jax
import jax.numpy as jnp
from jax import lax
from jax.experimental import pallas as pl
from jax.experimental.pallas import tpu as pltpu
from jax.sharding import PartitionSpec as P

damping = 0.1
N_CHUNK = 4
MESH = pl.DeviceIdType.MESH
f32 = jnp.float32
bf16 = jnp.bfloat16


def precondition(gradients, basis_in, basis_out, eigen_values):
    row_count = gradients.shape[0]
    grid_blocks = gradients.astype(jnp.float32).reshape(
        row_count, basis_out.shape[0], basis_in.shape[0]
    )
    rotated = jnp.einsum(
        "xi,qxy,yj->qij", basis_out, grid_blocks, basis_in, precision=lax.Precision.HIGHEST
    )
    scaled = rotated / (eigen_values + damping)
    restored = jnp.einsum(
        "bi,qij,aj->qba", basis_out, scaled, basis_in, precision=lax.Precision.HIGHEST
    )
    return restored.reshape(row_count, -1).astype(jnp.bfloat16)


def by_collectives(query_grads, stored_grads, basis_in, basis_out, eigen_values, layer_mask, doc_counts):
    stored = stored_grads[0]
    row_weights = layer_mask[:, 0].astype(jnp.bfloat16)
    own_rows = precondition(query_grads[0], basis_in[0], basis_out[0], eigen_values[0])
    masked = lax.all_gather(own_rows, "doc", axis=0, tiled=True) * row_weights[:, None]
    score_tiles = lax.dot_general(
        masked, stored, (((1,), (1,)), ((), ())), preferred_element_type=jnp.float32
    )
    live_slots = jnp.arange(stored.shape[0], dtype=jnp.int32) < doc_counts[0]
    score_tiles = jnp.where(live_slots[None, :], score_tiles, jnp.zeros_like(score_tiles))
    return lax.psum_scatter(score_tiles, "layer", scatter_dimension=0, tiled=True)


def halves(x):
    hi = x.astype(bf16)
    return hi, (x - hi.astype(f32)).astype(bf16)


def nn(a, b):
    return lax.dot_general(a, b, (((1,), (0,)), ((), ())), preferred_element_type=f32)


def nt(a, b):
    return lax.dot_general(a, b, (((1,), (1,)), ((), ())), preferred_element_type=f32)


def one_hot(hits):
    return jnp.where(hits, 1.0, 0.0).astype(bf16)


def iota(shape, dim):
    return lax.broadcasted_iota(jnp.int32, shape, dim)


def stacked(x):
    hi, lo = halves(x)
    return jnp.concatenate([hi, lo, hi], axis=0)


def write_own_rows(q_ref, bi_ref, bo_ref, ev_ref, mask_ref, xs, gath, me, ready, send_rows):
    for j in range(32):
        xs[32 * j : 32 * j + 32, :] = q_ref[0, :, 128 * j : 128 * j + 128].astype(f32)
    r, c = iota((256, 256), 0), iota((256, 256), 1)
    same = (r // 128 == (c // 64) % 2) & ((r // 64) % 2 == c // 128)
    put_a = one_hot(iota((256, 64), 0) % 64 == iota((256, 64), 1))
    wa = [
        jnp.where(same, nt(nn(put_a, part).astype(bf16), put_a), 0.0).astype(bf16)
        for part in halves(bi_ref[0])
    ]
    row = iota((64, 64), 0)
    put_b = one_hot(2 * (row % 32) + row // 32 == iota((64, 64), 1))
    col = iota((192, 64), 0)
    order = 2 * (col % 32) + (col // 32) % 2 == iota((192, 64), 1)
    place = [one_hot(order & (col < 128)), one_hot(order & (col >= 128))]
    wb, wc = 0.0, 0.0
    for part, to in zip(halves(bo_ref[0]), place):
        wb = wb + nt(nt(put_b, part).astype(bf16), to)
        wc = wc + nt(nn(put_b, part).astype(bf16), to)
    wb, wc = wb.astype(bf16), wc.astype(bf16)
    inverse = 1.0 / (ev_ref[0] + damping)
    top = inverse.astype(bf16)
    scale = 0.0
    for part in (top,) + halves(inverse - top.astype(f32)):
        scale = scale + nt(nn(put_b, part).astype(bf16), put_a[:128])
    scale = jnp.concatenate([scale] * 16, axis=1)

    block = jnp.concatenate(
        [
            jnp.concatenate(
                [xs[pl.ds(q + 16 * g, 32, stride=32), :] for g in range(2)], axis=1
            )
            for q in range(16)
        ],
        axis=0,
    ).astype(bf16)
    turned = nn(block, wa[0]) + nn(block, wa[1])
    s = jnp.concatenate(
        [
            jnp.concatenate(
                [turned[32 * q : 32 * q + 32, 128 * p : 128 * p + 128] for p in range(2)], axis=0
            )
            for q in range(16)
        ],
        axis=1,
    )
    rotated = nn(wb, stacked(s))
    v = nn(wc, stacked(rotated * scale))
    y = jnp.concatenate(
        [
            jnp.concatenate(
                [v[32 * p : 32 * p + 32, 128 * q : 128 * q + 128] for p in range(2)], axis=1
            )
            for q in range(16)
        ],
        axis=0,
    )
    y_hi, y_lo = halves(y)
    done = nt(y_hi, wa[0]) + (nt(y_lo, wa[0]) + nt(y_hi, wa[1]))
    for q in range(16):
        for g in range(2):
            xs[pl.ds(q + 16 * g, 32, stride=32), :] = done[
                32 * q : 32 * q + 32, 128 * g : 128 * g + 128
            ]
    picked = iota((32, 256), 1) == me * 32 + iota((32, 256), 0)
    weights = jnp.sum(jnp.where(picked, mask_ref[...].astype(f32), 0.0), axis=1, keepdims=True)
    rows = pl.ds(pl.multiple_of(me * 32, 32), 32)
    ready()

    def chunk(k, carry):
        for j in range(8):
            tile = xs[pl.ds(pl.multiple_of(256 * k + 32 * j, 32), 32), :]
            gath[k, rows, 128 * j : 128 * j + 128] = (tile * weights).astype(bf16)
        send_rows(k)
        return carry

    lax.fori_loop(0, N_CHUNK, chunk, 0)


def kernel(
    nz, q_ref, stored_ref, bi_ref, bo_ref, ev_ref, mask_ref, out_ref,
    xs, st, gath, acc, own, sbuf, rbuf, hbuf,
    st_sem, recv_sem, up_sem, down_sem, y_sem, rs_send, rs_recv, h_recv, out_sem,
):
    layers = sbuf.shape[0]
    width = st.shape[2]
    parts = sbuf.shape[1]
    me = lax.axis_index("doc")
    mine = lax.axis_index("layer")
    z, y = me // 2, me % 2
    partner = me + 1 - 2 * y

    def load(k):
        return pltpu.make_async_copy(
            stored_ref.at[0, :, pl.ds(k * width, width)], st.at[k], st_sem.at[k]
        )

    for k in range(N_CHUNK):
        load(k).start()

    barrier = pltpu.get_barrier_semaphore()
    pl.semaphore_signal(barrier, inc=1, device_id={"doc": partner}, device_id_type=MESH)
    for step in range(1, layers):
        pl.semaphore_signal(
            barrier, inc=1, device_id={"layer": lax.rem(mine + step, layers)}, device_id_type=MESH
        )

    @pl.when(z < nz - 1)
    def _():
        pl.semaphore_signal(barrier, inc=1, device_id={"doc": me + 2}, device_id_type=MESH)

    @pl.when(z > 0)
    def _():
        pl.semaphore_signal(barrier, inc=1, device_id={"doc": me - 2}, device_id_type=MESH)

    def plane_at(s):
        far = (z >= 2).astype(jnp.int32)
        near = z + far * (3 - 2 * z)
        inner = (near == 1).astype(jnp.int32)
        swap = inner * jnp.where(s < 2, 1, 0)
        p = s + swap * (1 - 2 * s)
        return p + far * (3 - 2 * p)

    def send(p, side, k, sems, target):
        blk = 2 * p + side
        part = gath.at[k, pl.ds(pl.multiple_of(blk * 32, 32), 32)]
        return pltpu.make_async_remote_copy(
            src_ref=part, dst_ref=part, send_sem=sems.at[blk, k], recv_sem=recv_sem.at[blk, k],
            device_id={"doc": target}, device_id_type=MESH,
        )

    def up(p, side, k):
        return send(p, side, k, up_sem, me + 2)

    def down(p, side, k):
        return send(p, side, k, down_sem, me - 2)

    def across(p, k):
        return send(p, y, k, y_sem, partner)

    def landed(p, side, k):
        return send(p, side, k, y_sem, partner)

    def both_columns(p, k):
        return ((p == 0) | (p == nz - 1)) & (k % 2 == 1)

    def goes_up(p):
        return (p <= z) & (z < nz - 1)

    def goes_down(p):
        return (p >= z) & (z > 0)

    def goes_across(p, k):
        return (p == z) | jnp.logical_not(both_columns(p, k))

    def relayed(p, k):
        return both_columns(p, k) & (p != z) & (p + z != nz - 1)

    def forward(t):
        p, k = plane_at(t // N_CHUNK), t % N_CHUNK

        landed(p, y, k).wait_recv()

        @pl.when(goes_up(p))
        def _():
            up(p, y, k).start()

        @pl.when(goes_down(p))
        def _():
            down(p, y, k).start()

        @pl.when(jnp.logical_not(both_columns(p, k)))
        def _():
            across(p, k).start()

    def send_rows(k):
        @pl.when(z < nz - 1)
        def _():
            up(z, y, k).start()

        @pl.when(z > 0)
        def _():
            down(z, y, k).start()

        across(z, k).start()

    def ready():
        ends = jnp.where(z == 0, 1, 0) + jnp.where(z == nz - 1, 1, 0)
        pl.semaphore_wait(barrier, layers + 2 - ends)

    def pass_on(p, k):
        @pl.when(goes_up(p))
        def _():
            up(p, 1 - y, k).start()

        @pl.when(goes_down(p))
        def _():
            down(p, 1 - y, k).start()

    def relay(t):
        p, k = plane_at(t // N_CHUNK), t % N_CHUNK

        @pl.when(relayed(p, k))
        def _():
            landed(p, 1 - y, k).wait_recv()
            pass_on(p, k)

    chip, core = mine // 2, mine % 2
    sibling = 2 * chip + 1 - core
    opposite = 2 * (1 - chip) + core

    def sums_for(p):
        return p == opposite

    def helps(p):
        return p == 2 * (1 - chip) + 1 - core

    def hand_over(p, s, n):
        return pltpu.make_async_remote_copy(
            src_ref=sbuf.at[s, n], dst_ref=rbuf.at[chip, n], send_sem=rs_send.at[s, n],
            recv_sem=rs_recv.at[chip, n], device_id={"layer": p}, device_id_type=MESH,
        )

    def help_out(s, n):
        return pltpu.make_async_remote_copy(
            src_ref=sbuf.at[s, n], dst_ref=hbuf.at[n], send_sem=rs_send.at[s, n],
            recv_sem=h_recv.at[n], device_id={"layer": sibling}, device_id_type=MESH,
        )

    def compute(t):
        s, k = t // N_CHUNK, t % N_CHUNK
        p = plane_at(s)

        @pl.when(jnp.logical_not(relayed(p, k)))
        def _():
            landed(p, 1 - y, k).wait_recv()

        @pl.when((s == 0) & both_columns(p, k))
        def _():
            pass_on(p, k)

        @pl.when(s == 0)
        def _():
            load(k).wait()

        rows = pl.ds(pl.multiple_of(p * 64, 64), 64)

        @pl.when(k == 0)
        def _():
            acc[...] = jnp.zeros_like(acc)

        @pl.when(k < N_CHUNK - 1)
        def _():
            acc[...] += nt(gath[k, rows, :], st[k])

        @pl.when(k == N_CHUNK - 1)
        def _():
            def column(n, carry):
                cols = pl.ds(pl.multiple_of(n * 256, 256), 256)
                total = acc[:, cols] + nt(gath[k, rows, :], st[k, cols, :])

                @pl.when(p == mine)
                def _():
                    own[:, cols] = total

                @pl.when(sums_for(p))
                def _():
                    acc[:, cols] = total

                @pl.when(p == sibling)
                def _():
                    sbuf[s, n] = total.astype(bf16)
                    hand_over(p, s, n).start()

                @pl.when(helps(p))
                def _():
                    sbuf[s, n] = total.astype(bf16)
                    help_out(s, n).start()

                return carry

            lax.fori_loop(0, parts, column, 0)

        @pl.when((k == N_CHUNK - 1) & sums_for(p))
        def _():
            def add(n, carry):
                cols = pl.ds(pl.multiple_of(n * 256, 256), 256)
                help_out(s, n).wait_recv()
                sbuf[s, n] = (acc[:, cols] + hbuf[n].astype(f32)).astype(bf16)
                hand_over(p, s, n).start()
                return carry

            lax.fori_loop(0, parts, add, 0)

    steps = nz * N_CHUNK

    def first(t, carry):
        forward(t)
        return carry

    def body(t, carry):
        @pl.when(t + lead < steps)
        def _():
            forward(t + lead)

        @pl.when(t + 2 < steps)
        def _():
            relay(t + 2)

        compute(t)
        return carry

    write_own_rows(q_ref, bi_ref, bo_ref, ev_ref, mask_ref, xs, gath, me, ready, send_rows)
    lead = N_CHUNK * jnp.where((z == 0) | (z == nz - 1), 1, 2)
    lax.fori_loop(N_CHUNK, lead, first, 0)
    lax.fori_loop(0, steps, body, 0)

    def drain(t, carry):
        p, k = t // N_CHUNK, t % N_CHUNK

        @pl.when(goes_up(p))
        def _():
            up(p, y, k).wait_send()

        @pl.when(goes_down(p))
        def _():
            down(p, y, k).wait_send()

        @pl.when(both_columns(p, k) & goes_up(p))
        def _():
            up(p, 1 - y, k).wait_send()

        @pl.when(both_columns(p, k) & goes_down(p))
        def _():
            down(p, 1 - y, k).wait_send()

        @pl.when(goes_across(p, k))
        def _():
            across(p, k).wait_send()

        return carry

    lax.fori_loop(0, steps, drain, 0)

    def drain_scores(t, carry):
        s, n = t // parts, t % parts
        p = plane_at(s)

        @pl.when(p != mine)
        def _():
            hand_over(p, s, n).wait_send()

        return carry

    lax.fori_loop(0, nz * parts, drain_scores, 0)

    def write(n):
        cols = pl.ds(n * 256 if isinstance(n, int) else pl.multiple_of(n * 256, 256), 256)
        return pltpu.make_async_copy(own.at[:, cols], out_ref.at[:, cols], out_sem.at[n])

    def collect(n, carry):
        cols = pl.ds(pl.multiple_of(n * 256, 256), 256)
        total = own[:, cols]
        for slot in range(2):
            pltpu.make_async_remote_copy(
                src_ref=sbuf.at[0, n], dst_ref=rbuf.at[slot, n], send_sem=rs_send.at[0, n],
                recv_sem=rs_recv.at[slot, n], device_id={"layer": sibling}, device_id_type=MESH,
            ).wait_recv()
            total = total + rbuf[slot, n].astype(f32)
        own[:, cols] = total
        write(n).start()
        return carry

    lax.fori_loop(0, parts, collect, 0)
    for n in range(parts):
        write(n).wait()


def in_one_kernel(nz, query_grads, stored_grads, basis_in, basis_out, eigen_values, layer_mask, doc_counts):
    layers = nz
    _, docs, depth = stored_grads.shape
    queries = layer_mask.shape[0]
    rows = queries // layers
    width = depth // N_CHUNK
    vmem = pl.BlockSpec(memory_space=pltpu.VMEM)
    summed = pl.pallas_call(
        functools.partial(kernel, nz),
        out_shape=jax.ShapeDtypeStruct((rows, docs), f32),
        in_specs=[vmem, pl.BlockSpec(memory_space=pltpu.HBM), vmem, vmem, vmem, vmem],
        out_specs=pl.BlockSpec(memory_space=pl.ANY),
        scratch_shapes=[
            pltpu.VMEM((depth * query_grads.shape[1] // 128, 128), f32),
            pltpu.VMEM((N_CHUNK, docs, width), bf16),
            pltpu.VMEM((N_CHUNK, queries, width), bf16),
            pltpu.VMEM((rows, docs), f32),
            pltpu.VMEM((rows, docs), f32),
            pltpu.VMEM((nz, docs // 256, rows, 256), bf16),
            pltpu.VMEM((2, docs // 256, rows, 256), bf16),
            pltpu.VMEM((docs // 256, rows, 256), bf16),
            pltpu.SemaphoreType.DMA((N_CHUNK,)),
            pltpu.SemaphoreType.DMA((2 * nz, N_CHUNK)),
            pltpu.SemaphoreType.DMA((2 * nz, N_CHUNK)),
            pltpu.SemaphoreType.DMA((2 * nz, N_CHUNK)),
            pltpu.SemaphoreType.DMA((2 * nz, N_CHUNK)),
            pltpu.SemaphoreType.DMA((nz, docs // 256)),
            pltpu.SemaphoreType.DMA((2, docs // 256)),
            pltpu.SemaphoreType.DMA((docs // 256,)),
            pltpu.SemaphoreType.DMA((docs // 256,)),
        ],
        compiler_params=pltpu.CompilerParams(
            collective_id=0, has_side_effects=True, vmem_limit_bytes=58 * 1024 * 1024
        ),
        cost_estimate=pl.CostEstimate(
            flops=2 * queries * docs * depth, bytes_accessed=2 * docs * depth, transcendentals=0
        ),
    )(query_grads, stored_grads, basis_in, basis_out, eigen_values, layer_mask.reshape(1, queries))
    live_slots = jnp.arange(docs, dtype=jnp.int32) < doc_counts[0]
    return jnp.where(live_slots[None, :], summed, jnp.zeros_like(summed))


def on_device(query_grads, stored_grads, *rest):
    n_doc, layers = lax.axis_size("doc"), lax.axis_size("layer")
    shape = query_grads.shape
    if n_doc == 8 and layers == 4 and shape == (1, 32, 4096):
        return in_one_kernel(n_doc // 2, query_grads, stored_grads, *rest)
    return by_collectives(query_grads, stored_grads, *rest)


def solution(mesh):
    in_specs = (
        P("layer", "doc", None),
        P("layer", "doc", None),
        P("layer", None, None),
        P("layer", None, None),
        P("layer", None, None),
        P(None, "layer"),
        P("doc"),
    )
    out_specs = P("layer", "doc")
    return jax.shard_map(
        on_device, mesh=mesh, in_specs=in_specs, out_specs=out_specs, check_vma=False
    )
```

```python
import functools
import jax
import jax.numpy as jnp
from jax import lax
from jax.experimental import pallas as pl
from jax.experimental.pallas import tpu as pltpu
from jax.sharding import PartitionSpec as P

damping = 0.1
N_CHUNK = 4
MESH = pl.DeviceIdType.MESH
f32 = jnp.float32
bf16 = jnp.bfloat16


def precondition(gradients, basis_in, basis_out, eigen_values):
    row_count = gradients.shape[0]
    grid_blocks = gradients.astype(jnp.float32).reshape(
        row_count, basis_out.shape[0], basis_in.shape[0]
    )
    rotated = jnp.einsum(
        "xi,qxy,yj->qij", basis_out, grid_blocks, basis_in, precision=lax.Precision.HIGHEST
    )
    scaled = rotated / (eigen_values + damping)
    restored = jnp.einsum(
        "bi,qij,aj->qba", basis_out, scaled, basis_in, precision=lax.Precision.HIGHEST
    )
    return restored.reshape(row_count, -1).astype(jnp.bfloat16)


def by_collectives(query_grads, stored_grads, basis_in, basis_out, eigen_values, layer_mask, doc_counts):
    stored = stored_grads[0]
    row_weights = layer_mask[:, 0].astype(jnp.bfloat16)
    own_rows = precondition(query_grads[0], basis_in[0], basis_out[0], eigen_values[0])
    masked = lax.all_gather(own_rows, "doc", axis=0, tiled=True) * row_weights[:, None]
    score_tiles = lax.dot_general(
        masked, stored, (((1,), (1,)), ((), ())), preferred_element_type=jnp.float32
    )
    live_slots = jnp.arange(stored.shape[0], dtype=jnp.int32) < doc_counts[0]
    score_tiles = jnp.where(live_slots[None, :], score_tiles, jnp.zeros_like(score_tiles))
    return lax.psum_scatter(score_tiles, "layer", scatter_dimension=0, tiled=True)


def halves(x):
    hi = x.astype(bf16)
    return hi, (x - hi.astype(f32)).astype(bf16)


def nn(a, b):
    return lax.dot_general(a, b, (((1,), (0,)), ((), ())), preferred_element_type=f32)


def nt(a, b):
    return lax.dot_general(a, b, (((1,), (1,)), ((), ())), preferred_element_type=f32)


def one_hot(hits):
    return jnp.where(hits, 1.0, 0.0).astype(bf16)


def iota(shape, dim):
    return lax.broadcasted_iota(jnp.int32, shape, dim)


def stacked(x):
    hi, lo = halves(x)
    return jnp.concatenate([hi, lo, hi], axis=0)


def write_own_rows(q_ref, bi_ref, bo_ref, ev_ref, mask_ref, xs, gath, me, ready, send_rows):
    for j in range(32):
        xs[32 * j : 32 * j + 32, :] = q_ref[0, :, 128 * j : 128 * j + 128].astype(f32)
    r, c = iota((256, 256), 0), iota((256, 256), 1)
    same = (r // 128 == (c // 64) % 2) & ((r // 64) % 2 == c // 128)
    put_a = one_hot(iota((256, 64), 0) % 64 == iota((256, 64), 1))
    wa = [
        jnp.where(same, nt(nn(put_a, part).astype(bf16), put_a), 0.0).astype(bf16)
        for part in halves(bi_ref[0])
    ]
    row = iota((64, 64), 0)
    put_b = one_hot(2 * (row % 32) + row // 32 == iota((64, 64), 1))
    col = iota((192, 64), 0)
    order = 2 * (col % 32) + (col // 32) % 2 == iota((192, 64), 1)
    place = [one_hot(order & (col < 128)), one_hot(order & (col >= 128))]
    wb, wc = 0.0, 0.0
    for part, to in zip(halves(bo_ref[0]), place):
        wb = wb + nt(nt(put_b, part).astype(bf16), to)
        wc = wc + nt(nn(put_b, part).astype(bf16), to)
    wb, wc = wb.astype(bf16), wc.astype(bf16)
    inverse = 1.0 / (ev_ref[0] + damping)
    top = inverse.astype(bf16)
    scale = 0.0
    for part in (top,) + halves(inverse - top.astype(f32)):
        scale = scale + nt(nn(put_b, part).astype(bf16), put_a[:128])
    scale = jnp.concatenate([scale] * 16, axis=1)

    block = jnp.concatenate(
        [
            jnp.concatenate(
                [xs[pl.ds(q + 16 * g, 32, stride=32), :] for g in range(2)], axis=1
            )
            for q in range(16)
        ],
        axis=0,
    ).astype(bf16)
    turned = nn(block, wa[0]) + nn(block, wa[1])
    s = jnp.concatenate(
        [
            jnp.concatenate(
                [turned[32 * q : 32 * q + 32, 128 * p : 128 * p + 128] for p in range(2)], axis=0
            )
            for q in range(16)
        ],
        axis=1,
    )
    rotated = nn(wb, stacked(s))
    v = nn(wc, stacked(rotated * scale))
    y = jnp.concatenate(
        [
            jnp.concatenate(
                [v[32 * p : 32 * p + 32, 128 * q : 128 * q + 128] for p in range(2)], axis=1
            )
            for q in range(16)
        ],
        axis=0,
    )
    y_hi, y_lo = halves(y)
    done = nt(y_hi, wa[0]) + (nt(y_lo, wa[0]) + nt(y_hi, wa[1]))
    for q in range(16):
        for g in range(2):
            xs[pl.ds(q + 16 * g, 32, stride=32), :] = done[
                32 * q : 32 * q + 32, 128 * g : 128 * g + 128
            ]
    picked = iota((32, 256), 1) == me * 32 + iota((32, 256), 0)
    weights = jnp.sum(jnp.where(picked, mask_ref[...].astype(f32), 0.0), axis=1, keepdims=True)
    rows = pl.ds(pl.multiple_of(me * 32, 32), 32)
    ready()

    def chunk(k, carry):
        for j in range(8):
            tile = xs[pl.ds(pl.multiple_of(256 * k + 32 * j, 32), 32), :]
            gath[k, rows, 128 * j : 128 * j + 128] = (tile * weights).astype(bf16)
        send_rows(k)
        return carry

    lax.fori_loop(0, N_CHUNK, chunk, 0)


def kernel(
    nz, q_ref, stored_ref, bi_ref, bo_ref, ev_ref, mask_ref, out_ref,
    xs, st, gath, acc, own, sbuf, rbuf,
    st_sem, recv_sem, up_sem, down_sem, y_sem, rs_send, rs_recv, out_sem,
):
    layers = sbuf.shape[0]
    width = st.shape[2]
    parts = sbuf.shape[1]
    me = lax.axis_index("doc")
    mine = lax.axis_index("layer")
    z, y = me // 2, me % 2
    partner = me + 1 - 2 * y

    def load(k):
        return pltpu.make_async_copy(
            stored_ref.at[0, :, pl.ds(k * width, width)], st.at[k], st_sem.at[k]
        )

    for k in range(N_CHUNK):
        load(k).start()

    barrier = pltpu.get_barrier_semaphore()
    pl.semaphore_signal(barrier, inc=1, device_id={"doc": partner}, device_id_type=MESH)
    for step in range(1, layers):
        pl.semaphore_signal(
            barrier, inc=1, device_id={"layer": lax.rem(mine + step, layers)}, device_id_type=MESH
        )

    @pl.when(z < nz - 1)
    def _():
        pl.semaphore_signal(barrier, inc=1, device_id={"doc": me + 2}, device_id_type=MESH)

    @pl.when(z > 0)
    def _():
        pl.semaphore_signal(barrier, inc=1, device_id={"doc": me - 2}, device_id_type=MESH)

    def plane_at(s):
        far = (z >= 2).astype(jnp.int32)
        near = z + far * (3 - 2 * z)
        inner = (near == 1).astype(jnp.int32)
        swap = inner * jnp.where(s < 2, 1, 0)
        p = s + swap * (1 - 2 * s)
        return p + far * (3 - 2 * p)

    def send(p, side, k, sems, target):
        blk = 2 * p + side
        part = gath.at[k, pl.ds(pl.multiple_of(blk * 32, 32), 32)]
        return pltpu.make_async_remote_copy(
            src_ref=part, dst_ref=part, send_sem=sems.at[blk, k], recv_sem=recv_sem.at[blk, k],
            device_id={"doc": target}, device_id_type=MESH,
        )

    def up(p, side, k):
        return send(p, side, k, up_sem, me + 2)

    def down(p, side, k):
        return send(p, side, k, down_sem, me - 2)

    def across(p, k):
        return send(p, y, k, y_sem, partner)

    def landed(p, side, k):
        return send(p, side, k, y_sem, partner)

    def both_columns(p, k):
        return ((p == 0) | (p == nz - 1)) & (k % 2 == 1)

    def goes_up(p):
        return (p <= z) & (z < nz - 1)

    def goes_down(p):
        return (p >= z) & (z > 0)

    def goes_across(p, k):
        return (p == z) | jnp.logical_not(both_columns(p, k))

    def relayed(p, k):
        return both_columns(p, k) & (p != z) & (p + z != nz - 1)

    def forward(t):
        p, k = plane_at(t // N_CHUNK), t % N_CHUNK

        landed(p, y, k).wait_recv()

        @pl.when(goes_up(p))
        def _():
            up(p, y, k).start()

        @pl.when(goes_down(p))
        def _():
            down(p, y, k).start()

        @pl.when(jnp.logical_not(both_columns(p, k)))
        def _():
            across(p, k).start()

    def send_rows(k):
        @pl.when(z < nz - 1)
        def _():
            up(z, y, k).start()

        @pl.when(z > 0)
        def _():
            down(z, y, k).start()

        across(z, k).start()

    def ready():
        ends = jnp.where(z == 0, 1, 0) + jnp.where(z == nz - 1, 1, 0)
        pl.semaphore_wait(barrier, layers + 2 - ends)

    def pass_on(p, k):
        @pl.when(goes_up(p))
        def _():
            up(p, 1 - y, k).start()

        @pl.when(goes_down(p))
        def _():
            down(p, 1 - y, k).start()

    def relay(t):
        p, k = plane_at(t // N_CHUNK), t % N_CHUNK

        @pl.when(relayed(p, k))
        def _():
            landed(p, 1 - y, k).wait_recv()
            pass_on(p, k)

    def hand_over(p, s, n):
        return pltpu.make_async_remote_copy(
            src_ref=sbuf.at[s, n], dst_ref=rbuf.at[mine, n], send_sem=rs_send.at[s, n],
            recv_sem=rs_recv.at[mine, n], device_id={"layer": p}, device_id_type=MESH,
        )

    def compute(t):
        s, k = t // N_CHUNK, t % N_CHUNK
        p = plane_at(s)

        @pl.when(jnp.logical_not(relayed(p, k)))
        def _():
            landed(p, 1 - y, k).wait_recv()

        @pl.when((s == 0) & both_columns(p, k))
        def _():
            pass_on(p, k)

        @pl.when(s == 0)
        def _():
            load(k).wait()

        rows = pl.ds(pl.multiple_of(p * 64, 64), 64)

        @pl.when(k == 0)
        def _():
            acc[...] = jnp.zeros_like(acc)

        @pl.when(k < N_CHUNK - 1)
        def _():
            acc[...] += nt(gath[k, rows, :], st[k])

        @pl.when(k == N_CHUNK - 1)
        def _():
            def column(n, carry):
                cols = pl.ds(pl.multiple_of(n * 256, 256), 256)
                total = acc[:, cols] + nt(gath[k, rows, :], st[k, cols, :])

                @pl.when(p == mine)
                def _():
                    own[:, cols] = total

                @pl.when(p != mine)
                def _():
                    sbuf[s, n] = total.astype(bf16)
                    hand_over(p, s, n).start()

                return carry

            lax.fori_loop(0, parts, column, 0)

    steps = nz * N_CHUNK

    def first(t, carry):
        forward(t)
        return carry

    def body(t, carry):
        @pl.when(t + lead < steps)
        def _():
            forward(t + lead)

        @pl.when(t + 2 < steps)
        def _():
            relay(t + 2)

        compute(t)
        return carry

    write_own_rows(q_ref, bi_ref, bo_ref, ev_ref, mask_ref, xs, gath, me, ready, send_rows)
    lead = N_CHUNK * jnp.where((z == 0) | (z == nz - 1), 1, 2)
    lax.fori_loop(N_CHUNK, lead, first, 0)
    lax.fori_loop(0, steps, body, 0)

    def drain(t, carry):
        p, k = t // N_CHUNK, t % N_CHUNK

        @pl.when(goes_up(p))
        def _():
            up(p, y, k).wait_send()

        @pl.when(goes_down(p))
        def _():
            down(p, y, k).wait_send()

        @pl.when(both_columns(p, k) & goes_up(p))
        def _():
            up(p, 1 - y, k).wait_send()

        @pl.when(both_columns(p, k) & goes_down(p))
        def _():
            down(p, 1 - y, k).wait_send()

        @pl.when(goes_across(p, k))
        def _():
            across(p, k).wait_send()

        return carry

    lax.fori_loop(0, steps, drain, 0)

    def drain_scores(t, carry):
        s, n = t // parts, t % parts
        p = plane_at(s)

        @pl.when(p != mine)
        def _():
            hand_over(p, s, n).wait_send()

        return carry

    lax.fori_loop(0, nz * parts, drain_scores, 0)

    def write(n):
        cols = pl.ds(n * 256 if isinstance(n, int) else pl.multiple_of(n * 256, 256), 256)
        return pltpu.make_async_copy(own.at[:, cols], out_ref.at[:, cols], out_sem.at[n])

    def collect(n, carry):
        cols = pl.ds(pl.multiple_of(n * 256, 256), 256)
        total = own[:, cols]
        for step in range(1, layers):
            other = lax.rem(mine + step, layers)
            pltpu.make_async_remote_copy(
                src_ref=sbuf.at[0, n], dst_ref=rbuf.at[other, n], send_sem=rs_send.at[0, n],
                recv_sem=rs_recv.at[other, n], device_id={"layer": other}, device_id_type=MESH,
            ).wait_recv()
            total = total + rbuf[other, n].astype(f32)
        own[:, cols] = total
        write(n).start()
        return carry

    lax.fori_loop(0, parts, collect, 0)
    for n in range(parts):
        write(n).wait()


def in_one_kernel(nz, query_grads, stored_grads, basis_in, basis_out, eigen_values, layer_mask, doc_counts):
    layers = nz
    _, docs, depth = stored_grads.shape
    queries = layer_mask.shape[0]
    rows = queries // layers
    width = depth // N_CHUNK
    vmem = pl.BlockSpec(memory_space=pltpu.VMEM)
    summed = pl.pallas_call(
        functools.partial(kernel, nz),
        out_shape=jax.ShapeDtypeStruct((rows, docs), f32),
        in_specs=[vmem, pl.BlockSpec(memory_space=pltpu.HBM), vmem, vmem, vmem, vmem],
        out_specs=pl.BlockSpec(memory_space=pl.ANY),
        scratch_shapes=[
            pltpu.VMEM((depth * query_grads.shape[1] // 128, 128), f32),
            pltpu.VMEM((N_CHUNK, docs, width), bf16),
            pltpu.VMEM((N_CHUNK, queries, width), bf16),
            pltpu.VMEM((rows, docs), f32),
            pltpu.VMEM((rows, docs), f32),
            pltpu.VMEM((nz, docs // 256, rows, 256), bf16),
            pltpu.VMEM((layers, docs // 256, rows, 256), bf16),
            pltpu.SemaphoreType.DMA((N_CHUNK,)),
            pltpu.SemaphoreType.DMA((2 * nz, N_CHUNK)),
            pltpu.SemaphoreType.DMA((2 * nz, N_CHUNK)),
            pltpu.SemaphoreType.DMA((2 * nz, N_CHUNK)),
            pltpu.SemaphoreType.DMA((2 * nz, N_CHUNK)),
            pltpu.SemaphoreType.DMA((nz, docs // 256)),
            pltpu.SemaphoreType.DMA((layers, docs // 256)),
            pltpu.SemaphoreType.DMA((docs // 256,)),
        ],
        compiler_params=pltpu.CompilerParams(
            collective_id=0, has_side_effects=True, vmem_limit_bytes=58 * 1024 * 1024
        ),
        cost_estimate=pl.CostEstimate(
            flops=2 * queries * docs * depth, bytes_accessed=2 * docs * depth, transcendentals=0
        ),
    )(query_grads, stored_grads, basis_in, basis_out, eigen_values, layer_mask.reshape(1, queries))
    live_slots = jnp.arange(docs, dtype=jnp.int32) < doc_counts[0]
    return jnp.where(live_slots[None, :], summed, jnp.zeros_like(summed))


def on_device(query_grads, stored_grads, *rest):
    n_doc, layers = lax.axis_size("doc"), lax.axis_size("layer")
    shape = query_grads.shape
    if n_doc == 8 and layers == 4 and shape == (1, 32, 4096):
        return in_one_kernel(n_doc // 2, query_grads, stored_grads, *rest)
    return by_collectives(query_grads, stored_grads, *rest)


def solution(mesh):
    in_specs = (
        P("layer", "doc", None),
        P("layer", "doc", None),
        P("layer", None, None),
        P("layer", None, None),
        P("layer", None, None),
        P(None, "layer"),
        P("doc"),
    )
    out_specs = P("layer", "doc")
    return jax.shard_map(
        on_device, mesh=mesh, in_specs=in_specs, out_specs=out_specs, check_vma=False
    )
```

```python
import functools
import jax
import jax.numpy as jnp
from jax import lax
from jax.experimental import pallas as pl
from jax.experimental.pallas import tpu as pltpu
from jax.sharding import PartitionSpec as P

damping = 0.1
N_CHUNK = 8
MESH = pl.DeviceIdType.MESH
f32 = jnp.float32
bf16 = jnp.bfloat16


def precondition(gradients, basis_in, basis_out, eigen_values):
    row_count = gradients.shape[0]
    grid_blocks = gradients.astype(jnp.float32).reshape(
        row_count, basis_out.shape[0], basis_in.shape[0]
    )
    rotated = jnp.einsum(
        "xi,qxy,yj->qij", basis_out, grid_blocks, basis_in, precision=lax.Precision.HIGHEST
    )
    scaled = rotated / (eigen_values + damping)
    restored = jnp.einsum(
        "bi,qij,aj->qba", basis_out, scaled, basis_in, precision=lax.Precision.HIGHEST
    )
    return restored.reshape(row_count, -1).astype(jnp.bfloat16)


def by_collectives(query_grads, stored_grads, basis_in, basis_out, eigen_values, layer_mask, doc_counts):
    stored = stored_grads[0]
    row_weights = layer_mask[:, 0].astype(jnp.bfloat16)
    own_rows = precondition(query_grads[0], basis_in[0], basis_out[0], eigen_values[0])
    masked = lax.all_gather(own_rows, "doc", axis=0, tiled=True) * row_weights[:, None]
    score_tiles = lax.dot_general(
        masked, stored, (((1,), (1,)), ((), ())), preferred_element_type=jnp.float32
    )
    live_slots = jnp.arange(stored.shape[0], dtype=jnp.int32) < doc_counts[0]
    score_tiles = jnp.where(live_slots[None, :], score_tiles, jnp.zeros_like(score_tiles))
    return lax.psum_scatter(score_tiles, "layer", scatter_dimension=0, tiled=True)


def halves(x):
    hi = x.astype(bf16)
    return hi, (x - hi.astype(f32)).astype(bf16)


def nn(a, b):
    return lax.dot_general(a, b, (((1,), (0,)), ((), ())), preferred_element_type=f32)


def nt(a, b):
    return lax.dot_general(a, b, (((1,), (1,)), ((), ())), preferred_element_type=f32)


def one_hot(hits):
    return jnp.where(hits, 1.0, 0.0).astype(bf16)


def iota(shape, dim):
    return lax.broadcasted_iota(jnp.int32, shape, dim)


def stacked(x):
    hi, lo = halves(x)
    return jnp.concatenate([hi, lo, hi], axis=0)


def write_own_rows(q_ref, bi_ref, bo_ref, ev_ref, mask_ref, xs, gath, me, ready, send_rows):
    for j in range(32):
        xs[32 * j : 32 * j + 32, :] = q_ref[0, :, 128 * j : 128 * j + 128].astype(f32)
    r, c = iota((256, 256), 0), iota((256, 256), 1)
    same = (r // 128 == (c // 64) % 2) & ((r // 64) % 2 == c // 128)
    put_a = one_hot(iota((256, 64), 0) % 64 == iota((256, 64), 1))
    wa = [
        jnp.where(same, nt(nn(put_a, part).astype(bf16), put_a), 0.0).astype(bf16)
        for part in halves(bi_ref[0])
    ]
    row = iota((64, 64), 0)
    put_b = one_hot(2 * (row % 32) + row // 32 == iota((64, 64), 1))
    col = iota((192, 64), 0)
    order = 2 * (col % 32) + (col // 32) % 2 == iota((192, 64), 1)
    place = [one_hot(order & (col < 128)), one_hot(order & (col >= 128))]
    wb, wc = 0.0, 0.0
    for part, to in zip(halves(bo_ref[0]), place):
        wb = wb + nt(nt(put_b, part).astype(bf16), to)
        wc = wc + nt(nn(put_b, part).astype(bf16), to)
    wb, wc = wb.astype(bf16), wc.astype(bf16)
    inverse = 1.0 / (ev_ref[0] + damping)
    top = inverse.astype(bf16)
    scale = 0.0
    for part in (top,) + halves(inverse - top.astype(f32)):
        scale = scale + nt(nn(put_b, part).astype(bf16), put_a[:128])
    scale = jnp.concatenate([scale] * 16, axis=1)

    block = jnp.concatenate(
        [
            jnp.concatenate(
                [xs[pl.ds(q + 16 * g, 32, stride=32), :] for g in range(2)], axis=1
            )
            for q in range(16)
        ],
        axis=0,
    ).astype(bf16)
    turned = nn(block, wa[0]) + nn(block, wa[1])
    s = jnp.concatenate(
        [
            jnp.concatenate(
                [turned[32 * q : 32 * q + 32, 128 * p : 128 * p + 128] for p in range(2)], axis=0
            )
            for q in range(16)
        ],
        axis=1,
    )
    rotated = nn(wb, stacked(s))
    v = nn(wc, stacked(rotated * scale))
    y = jnp.concatenate(
        [
            jnp.concatenate(
                [v[32 * p : 32 * p + 32, 128 * q : 128 * q + 128] for p in range(2)], axis=1
            )
            for q in range(16)
        ],
        axis=0,
    )
    y_hi, y_lo = halves(y)
    done = nt(y_hi, wa[0]) + (nt(y_lo, wa[0]) + nt(y_hi, wa[1]))
    for q in range(16):
        for g in range(2):
            xs[pl.ds(q + 16 * g, 32, stride=32), :] = done[
                32 * q : 32 * q + 32, 128 * g : 128 * g + 128
            ]
    picked = iota((32, 256), 1) == me * 32 + iota((32, 256), 0)
    weights = jnp.sum(jnp.where(picked, mask_ref[...].astype(f32), 0.0), axis=1, keepdims=True)
    rows = pl.ds(pl.multiple_of(me * 32, 32), 32)
    ready()

    def chunk(k, carry):
        for j in range(32 // N_CHUNK):
            tile = xs[pl.ds(pl.multiple_of((1024 // N_CHUNK) * k + 32 * j, 32), 32), :]
            gath[k, rows, 128 * j : 128 * j + 128] = (tile * weights).astype(bf16)
        send_rows(k)
        return carry

    lax.fori_loop(0, N_CHUNK, chunk, 0)


def kernel(
    nz, q_ref, stored_ref, bi_ref, bo_ref, ev_ref, mask_ref, out_ref,
    xs, st, gath, acc, own, sbuf, rbuf,
    st_sem, recv_sem, up_sem, down_sem, y_sem, rs_send, rs_recv, out_sem,
):
    layers = sbuf.shape[0]
    width = st.shape[2]
    parts = sbuf.shape[1]
    me = lax.axis_index("doc")
    mine = lax.axis_index("layer")
    z, y = me // 2, me % 2
    partner = me + 1 - 2 * y

    def load(k):
        return pltpu.make_async_copy(
            stored_ref.at[0, :, pl.ds(k * width, width)], st.at[k], st_sem.at[k]
        )

    for k in range(N_CHUNK):
        load(k).start()

    barrier = pltpu.get_barrier_semaphore()
    pl.semaphore_signal(barrier, inc=1, device_id={"doc": partner}, device_id_type=MESH)
    for step in range(1, layers):
        pl.semaphore_signal(
            barrier, inc=1, device_id={"layer": lax.rem(mine + step, layers)}, device_id_type=MESH
        )

    @pl.when(z < nz - 1)
    def _():
        pl.semaphore_signal(barrier, inc=1, device_id={"doc": me + 2}, device_id_type=MESH)

    @pl.when(z > 0)
    def _():
        pl.semaphore_signal(barrier, inc=1, device_id={"doc": me - 2}, device_id_type=MESH)

    def plane_at(s):
        far = (z >= 2).astype(jnp.int32)
        near = z + far * (3 - 2 * z)
        inner = (near == 1).astype(jnp.int32)
        swap = inner * jnp.where(s < 2, 1, 0)
        p = s + swap * (1 - 2 * s)
        return p + far * (3 - 2 * p)

    def send(p, side, k, sems, target):
        blk = 2 * p + side
        part = gath.at[k, pl.ds(pl.multiple_of(blk * 32, 32), 32)]
        return pltpu.make_async_remote_copy(
            src_ref=part, dst_ref=part, send_sem=sems.at[blk, k], recv_sem=recv_sem.at[blk, k],
            device_id={"doc": target}, device_id_type=MESH,
        )

    def up(p, side, k):
        return send(p, side, k, up_sem, me + 2)

    def down(p, side, k):
        return send(p, side, k, down_sem, me - 2)

    def across(p, k):
        return send(p, y, k, y_sem, partner)

    def landed(p, side, k):
        return send(p, side, k, y_sem, partner)

    def both_columns(p, k):
        return ((p == 0) | (p == nz - 1)) & (k % 2 == 1)

    def goes_up(p):
        return (p <= z) & (z < nz - 1)

    def goes_down(p):
        return (p >= z) & (z > 0)

    def goes_across(p, k):
        return (p == z) | jnp.logical_not(both_columns(p, k))

    def relayed(p, k):
        return both_columns(p, k) & (p != z) & (p + z != nz - 1)

    def forward(t):
        p, k = plane_at(t // N_CHUNK), t % N_CHUNK

        landed(p, y, k).wait_recv()

        @pl.when(goes_up(p))
        def _():
            up(p, y, k).start()

        @pl.when(goes_down(p))
        def _():
            down(p, y, k).start()

        @pl.when(jnp.logical_not(both_columns(p, k)))
        def _():
            across(p, k).start()

    def send_rows(k):
        @pl.when(z < nz - 1)
        def _():
            up(z, y, k).start()

        @pl.when(z > 0)
        def _():
            down(z, y, k).start()

        across(z, k).start()

    def ready():
        ends = jnp.where(z == 0, 1, 0) + jnp.where(z == nz - 1, 1, 0)
        pl.semaphore_wait(barrier, layers + 2 - ends)

    def pass_on(p, k):
        @pl.when(goes_up(p))
        def _():
            up(p, 1 - y, k).start()

        @pl.when(goes_down(p))
        def _():
            down(p, 1 - y, k).start()

    def relay(t):
        p, k = plane_at(t // N_CHUNK), t % N_CHUNK

        @pl.when(relayed(p, k))
        def _():
            landed(p, 1 - y, k).wait_recv()
            pass_on(p, k)

    def hand_over(p, s, n):
        return pltpu.make_async_remote_copy(
            src_ref=sbuf.at[s, n], dst_ref=rbuf.at[mine, n], send_sem=rs_send.at[s, n],
            recv_sem=rs_recv.at[mine, n], device_id={"layer": p}, device_id_type=MESH,
        )

    def compute(t):
        s, k = t // N_CHUNK, t % N_CHUNK
        p = plane_at(s)

        @pl.when(jnp.logical_not(relayed(p, k)))
        def _():
            landed(p, 1 - y, k).wait_recv()

        @pl.when((s == 0) & both_columns(p, k))
        def _():
            pass_on(p, k)

        @pl.when(s == 0)
        def _():
            load(k).wait()

        rows = pl.ds(pl.multiple_of(p * 64, 64), 64)

        @pl.when(k == 0)
        def _():
            acc[...] = jnp.zeros_like(acc)

        @pl.when(k < N_CHUNK - 1)
        def _():
            acc[...] += nt(gath[k, rows, :], st[k])

        @pl.when(k == N_CHUNK - 1)
        def _():
            def column(n, carry):
                cols = pl.ds(pl.multiple_of(n * 256, 256), 256)
                total = acc[:, cols] + nt(gath[k, rows, :], st[k, cols, :])

                @pl.when(p == mine)
                def _():
                    own[:, cols] = total

                @pl.when(p != mine)
                def _():
                    sbuf[s, n] = total.astype(bf16)
                    hand_over(p, s, n).start()

                return carry

            lax.fori_loop(0, parts, column, 0)

    steps = nz * N_CHUNK

    def first(t, carry):
        forward(t)
        return carry

    def body(t, carry):
        @pl.when(t + lead < steps)
        def _():
            forward(t + lead)

        @pl.when(t + N_CHUNK // 2 < steps)
        def _():
            relay(t + N_CHUNK // 2)

        compute(t)
        return carry

    write_own_rows(q_ref, bi_ref, bo_ref, ev_ref, mask_ref, xs, gath, me, ready, send_rows)
    lead = N_CHUNK * jnp.where((z == 0) | (z == nz - 1), 1, 2)
    lax.fori_loop(N_CHUNK, lead, first, 0)
    lax.fori_loop(0, steps, body, 0)

    def drain(t, carry):
        p, k = t // N_CHUNK, t % N_CHUNK

        @pl.when(goes_up(p))
        def _():
            up(p, y, k).wait_send()

        @pl.when(goes_down(p))
        def _():
            down(p, y, k).wait_send()

        @pl.when(both_columns(p, k) & goes_up(p))
        def _():
            up(p, 1 - y, k).wait_send()

        @pl.when(both_columns(p, k) & goes_down(p))
        def _():
            down(p, 1 - y, k).wait_send()

        @pl.when(goes_across(p, k))
        def _():
            across(p, k).wait_send()

        return carry

    lax.fori_loop(0, steps, drain, 0)

    def drain_scores(t, carry):
        s, n = t // parts, t % parts
        p = plane_at(s)

        @pl.when(p != mine)
        def _():
            hand_over(p, s, n).wait_send()

        return carry

    lax.fori_loop(0, nz * parts, drain_scores, 0)

    def write(n):
        cols = pl.ds(n * 256 if isinstance(n, int) else pl.multiple_of(n * 256, 256), 256)
        return pltpu.make_async_copy(own.at[:, cols], out_ref.at[:, cols], out_sem.at[n])

    def collect(n, carry):
        cols = pl.ds(pl.multiple_of(n * 256, 256), 256)
        total = own[:, cols]
        for step in range(1, layers):
            other = lax.rem(mine + step, layers)
            pltpu.make_async_remote_copy(
                src_ref=sbuf.at[0, n], dst_ref=rbuf.at[other, n], send_sem=rs_send.at[0, n],
                recv_sem=rs_recv.at[other, n], device_id={"layer": other}, device_id_type=MESH,
            ).wait_recv()
            total = total + rbuf[other, n].astype(f32)
        own[:, cols] = total
        write(n).start()
        return carry

    lax.fori_loop(0, parts, collect, 0)
    for n in range(parts):
        write(n).wait()


def in_one_kernel(nz, query_grads, stored_grads, basis_in, basis_out, eigen_values, layer_mask, doc_counts):
    layers = nz
    _, docs, depth = stored_grads.shape
    queries = layer_mask.shape[0]
    rows = queries // layers
    width = depth // N_CHUNK
    vmem = pl.BlockSpec(memory_space=pltpu.VMEM)
    summed = pl.pallas_call(
        functools.partial(kernel, nz),
        out_shape=jax.ShapeDtypeStruct((rows, docs), f32),
        in_specs=[vmem, pl.BlockSpec(memory_space=pltpu.HBM), vmem, vmem, vmem, vmem],
        out_specs=pl.BlockSpec(memory_space=pl.ANY),
        scratch_shapes=[
            pltpu.VMEM((depth * query_grads.shape[1] // 128, 128), f32),
            pltpu.VMEM((N_CHUNK, docs, width), bf16),
            pltpu.VMEM((N_CHUNK, queries, width), bf16),
            pltpu.VMEM((rows, docs), f32),
            pltpu.VMEM((rows, docs), f32),
            pltpu.VMEM((nz, docs // 256, rows, 256), bf16),
            pltpu.VMEM((layers, docs // 256, rows, 256), bf16),
            pltpu.SemaphoreType.DMA((N_CHUNK,)),
            pltpu.SemaphoreType.DMA((2 * nz, N_CHUNK)),
            pltpu.SemaphoreType.DMA((2 * nz, N_CHUNK)),
            pltpu.SemaphoreType.DMA((2 * nz, N_CHUNK)),
            pltpu.SemaphoreType.DMA((2 * nz, N_CHUNK)),
            pltpu.SemaphoreType.DMA((nz, docs // 256)),
            pltpu.SemaphoreType.DMA((layers, docs // 256)),
            pltpu.SemaphoreType.DMA((docs // 256,)),
        ],
        compiler_params=pltpu.CompilerParams(
            collective_id=0, has_side_effects=True, vmem_limit_bytes=58 * 1024 * 1024
        ),
        cost_estimate=pl.CostEstimate(
            flops=2 * queries * docs * depth, bytes_accessed=2 * docs * depth, transcendentals=0
        ),
    )(query_grads, stored_grads, basis_in, basis_out, eigen_values, layer_mask.reshape(1, queries))
    live_slots = jnp.arange(docs, dtype=jnp.int32) < doc_counts[0]
    return jnp.where(live_slots[None, :], summed, jnp.zeros_like(summed))


def on_device(query_grads, stored_grads, *rest):
    n_doc, layers = lax.axis_size("doc"), lax.axis_size("layer")
    shape = query_grads.shape
    if n_doc == 8 and layers == 4 and shape == (1, 32, 4096):
        return in_one_kernel(n_doc // 2, query_grads, stored_grads, *rest)
    return by_collectives(query_grads, stored_grads, *rest)


def solution(mesh):
    in_specs = (
        P("layer", "doc", None),
        P("layer", "doc", None),
        P("layer", None, None),
        P("layer", None, None),
        P("layer", None, None),
        P(None, "layer"),
        P("doc"),
    )
    out_specs = P("layer", "doc")
    return jax.shard_map(
        on_device, mesh=mesh, in_specs=in_specs, out_specs=out_specs, check_vma=False
    )
```
